512 devices in a mesh: freq: 32 (over z_hi, y, core), gx: 16 (over z_lo, x).
Axes of the slice: x: 4, y: 4, z: 16 (z_hi: 4, z_lo: 4; z = z_hi * 4 + z_lo), core: 2. Of those that a mesh axis runs over, the one named last changes fastest.
Arguments:
- wavefield: float32 [2, 64, 2048, 128], P(None, 'freq', 'gx'), may hold values from -6 to 6
- velocity_bank: float32 [32, 2048, 128], P('freq', 'gx'), may hold values from 1.5 to 4.5
- owner: int32 [1], replicated, may hold values from 0 to 31
Outputs:
- wave_out: float32 [2, 64, 2048, 128], P(None, 'freq', 'gx')
- stacked_image: float32 [2048, 128], P('gx')
The draws below stay inside these ranges and needn't reach their ends.
All inputs are finite; a program needn't handle non-finite values.
Results may differ from the reference program's by a relative error of at most 0.0015.
Values sent between devices are 32-bit elements; how exact they have to be, the bound alone decides.
No kernel may reach another device: no remote copies, remote signals or barrier semaphores. Data moves between devices by JAX's collectives and lax.ppermute only.
A program may use at most 64 MiB of HBM per device.

```python
import math
import jax
import jax.numpy as jnp
from jax import lax

NY = 128
STEPS = 1
NX = 2048
NF = 64
SLOTS = 32


def draw_wavefield(key, part):
    key = jax.random.fold_in(key, 11)
    rough_key = jax.random.fold_in(key, 0)
    return jnp.clip(jax.random.normal(rough_key, (2, NF, NX, NY), jnp.float32), -6.0, 6.0)


def shard_levels(key, extent, shards, least, high):
    gain = 1.0
    for position, shards_of in shards:
        draws = jax.random.uniform(jax.random.fold_in(jax.random.fold_in(key, 6), position), (shards_of,), jnp.float32, least / len(shards), high / len(shards))
        gain = gain * jnp.repeat(jnp.exp(draws), extent[position] // shards_of).reshape((-1,) + (1,) * (len(extent) - 1 - position))
    return gain


def setup_inputs(seed: int = 0) -> dict:
    key_of = jax.random.split(jax.random.key(seed), 4)
    return {
        "wavefield": draw_wavefield(jax.random.fold_in(key_of[3], 71), 0),
        "velocity_bank": jnp.clip(1.5 + 3.0 * jax.random.uniform(key_of[1], (SLOTS, NX, NY), jnp.float32) ** shard_levels(key_of[1], (SLOTS, NX, NY), ((0, 32), (1, 16)), -0.2, 0.2), 1.5, 4.5),
        "owner": jax.random.randint(key_of[2], (STEPS,), 0, SLOTS).astype(jnp.int32),
    }


BETA = 1.0 / 6.0
GAIN = 30000.0
PHASE = 2.0

def times_complex(left_re, left_im, right_re, right_im):
    return (left_re * right_re - left_im * right_im, left_re * right_im + left_im * right_re)

def divide_complex(top_re, top_im, bottom_re, bottom_im):
    denominator = bottom_re * bottom_re + bottom_im * bottom_im
    return ((top_re * bottom_re + top_im * bottom_im) / denominator, (top_im * bottom_re - top_re * bottom_im) / denominator)

def pack_system(members):
    return jnp.stack([jnp.stack([member[0], member[1]]) for member in members])

def build(wave_in, kappa_re, kappa_im, prev_rows, next_rows, head_mask, tail_mask):
    laplace = prev_rows - 2.0 * wave_in + next_rows
    right_re, right_im = times_complex(kappa_re, -kappa_im, laplace[0], laplace[1])
    return pack_system([(kappa_re * head_mask, kappa_im * head_mask), (-2.0 * kappa_re, -2.0 * kappa_im), (kappa_re * tail_mask, kappa_im * tail_mask), (wave_in[0] + right_re, wave_in[1] + right_im)])

def reduce_level(system, below, above):
    alpha_re, alpha_im = divide_complex(-system[0, 0], -system[0, 1], below[1, 0] + 1.0, below[1, 1])
    gamma_re, gamma_im = divide_complex(-system[2, 0], -system[2, 1], above[1, 0] + 1.0, above[1, 1])
    lower_coef = times_complex(alpha_re, alpha_im, below[0, 0], below[0, 1])
    upper_coef = times_complex(gamma_re, gamma_im, above[2, 0], above[2, 1])
    left_diag = times_complex(alpha_re, alpha_im, below[2, 0], below[2, 1])
    right_diag = times_complex(gamma_re, gamma_im, above[0, 0], above[0, 1])
    left_rhs = times_complex(alpha_re, alpha_im, below[3, 0], below[3, 1])
    right_rhs = times_complex(gamma_re, gamma_im, above[3, 0], above[3, 1])
    center = (system[1, 0] + left_diag[0] + right_diag[0], system[1, 1] + left_diag[1] + right_diag[1])
    source = (system[3, 0] + left_rhs[0] + right_rhs[0], system[3, 1] + left_rhs[1] + right_rhs[1])
    return pack_system([lower_coef, center, upper_coef, source])

def finish(system):
    sol_re, sol_im = divide_complex(system[3, 0], system[3, 1], system[1, 0] + 1.0, system[1, 1])
    return jnp.stack([sol_re, sol_im])

def rows_below(array, stride, axis):
    length = array.shape[axis]
    zeros_part = jnp.zeros_like(lax.slice_in_dim(array, 0, stride, axis=axis))
    return jnp.concatenate([zeros_part, lax.slice_in_dim(array, 0, length - stride, axis=axis)], axis=axis)

def rows_above(array, stride, axis):
    length = array.shape[axis]
    zeros_part = jnp.zeros_like(lax.slice_in_dim(array, 0, stride, axis=axis))
    return jnp.concatenate([lax.slice_in_dim(array, stride, length, axis=axis), zeros_part], axis=axis)

def local_solve(wave_in, kappa_re, kappa_im, axis):
    length = wave_in.shape[axis]
    shape_list = [1, 1, 1]
    shape_list[axis - 1] = length
    places = jnp.arange(length).reshape(shape_list)
    head_mask = (places > 0).astype(jnp.float32)
    tail_mask = (places < length - 1).astype(jnp.float32)
    system = build(wave_in, kappa_re, kappa_im, rows_below(wave_in, 1, axis), rows_above(wave_in, 1, axis), head_mask, tail_mask)
    stride = 1
    while stride < length:
        system = reduce_level(system, rows_below(system, stride, axis + 1), rows_above(system, stride, axis + 1))
        stride = stride * 2
    return finish(system)

def screen(wave_in, velocity, angular):
    angle_now = angular * PHASE * (1.0 / velocity - 1.0 / 3.0)
    new_re, new_im = times_complex(wave_in[0], wave_in[1], jnp.cos(angle_now), jnp.sin(angle_now))
    return jnp.stack([new_re, new_im])

def reference(wavefield, velocity_bank, owner):
    freq_count = wavefield.shape[1]
    angular = (1.0 + 3.0 * jnp.arange(freq_count).astype(jnp.float32) / freq_count).reshape(freq_count, 1, 1)
    wave_now = wavefield
    for depth_step in range(STEPS):
        velocity = lax.dynamic_index_in_dim(velocity_bank, owner[depth_step], 0, keepdims=False)
        wave_now = screen(wave_now, velocity, angular)
        kappa_im = -GAIN * velocity / angular
        kappa_re = jnp.full_like(kappa_im, BETA)
        wave_now = local_solve(wave_now, kappa_re, kappa_im, 2)
    stacked_image = lax.optimization_barrier(jnp.sum(wave_now[0], axis=0)) * (1.0 / math.sqrt(freq_count))
    return (wave_now, stacked_image)
```

```python
import functools
import math

import jax
import jax.numpy as jnp
from jax import lax
from jax.experimental import pallas as pl
from jax.experimental.pallas import tpu as pltpu
from jax.sharding import Mesh, PartitionSpec as P

BETA = 1.0 / 6.0
GAIN = 30000.0
PHASE = 2.0

ZH, YY, CC, ZL, XX = 4, 4, 2, 4, 4
FREQ = ("zh", "y", "c")
STRIPS = ("zl", "x")
N_STRIPS = ZL * XX
SEGMENTS = 8
FIELDS = 7
MESSAGE = 32


def mul(a, b):
    return (a[0] * b[0] - a[1] * b[1], a[0] * b[1] + a[1] * b[0])


def add(a, b):
    return (a[0] + b[0], a[1] + b[1])


def sub(a, b):
    return (a[0] - b[0], a[1] - b[1])


def neg(a):
    return (-a[0], -a[1])


def scale(s, a):
    return (s * a[0], s * a[1])


def reciprocal(a):
    inverse = 1.0 / (a[0] * a[0] + a[1] * a[1])
    return (a[0] * inverse, -a[1] * inverse)


def sin_cos(angle):
    h = 0.5 * angle
    z = h * h
    s = 1.0 / 6227020800.0
    for k in (-1.0 / 39916800.0, 1.0 / 362880.0, -1.0 / 5040.0, 1.0 / 120.0, -1.0 / 6.0):
        s = s * z + k
    s = h + h * (z * s)
    c = 1.0 / 87178291200.0
    c = -c * z + 1.0 / 479001600.0
    for k in (-1.0 / 3628800.0, 1.0 / 40320.0, -1.0 / 720.0, 1.0 / 24.0, -0.5):
        c = c * z + k
    c = 1.0 + z * c
    return 2.0 * s * c, 1.0 - 2.0 * s * s


def inverse_kappa(velocity, angular):
    big = GAIN * velocity * (1.0 / angular)
    inverse = 1.0 / (BETA * BETA + big * big)
    return (BETA * inverse, big * inverse)


def angular_of(f, freq_local, freq_total):
    index = (lax.axis_index("zh") * YY + lax.axis_index("y")) * CC + lax.axis_index("c")
    index = index * freq_local + f
    return 1.0 + 3.0 * index.astype(jnp.float32) / freq_total


def shift_rows(x, distance, rows):
    count = x.shape[0]
    rolled = pltpu.roll(x, distance % count, 0)
    inside = rows >= distance if distance > 0 else rows < count + distance
    return jnp.where(inside, rolled, 0.0)


def shift_pair(a, distance, rows):
    return (shift_rows(a[0], distance, rows), shift_rows(a[1], distance, rows))


def source_terms(wave, t, steps, eps, rows):
    here = wave(t)
    prev = wave(t - 1) if t > 0 else shift_pair(wave(steps - 1), 1, rows)
    after = wave(t + 1) if t < steps - 1 else shift_pair(wave(0), -1, rows)
    lap = sub(add(prev, after), scale(2.0, here))
    return mul(scale(2.0, eps), add(here, scale(BETA, lap)))


def forward_kernel(freq_total, owner_ref, wave_ref, vel_ref, screened_ref, scan_ref, message_ref, rows_ref):
    freq_local, cells = wave_ref.shape[1], wave_ref.shape[2]
    steps = cells // SEGMENTS
    lanes = wave_ref.shape[3]
    core = lax.rem(owner_ref[0], CC)
    rows = lax.broadcasted_iota(jnp.int32, (SEGMENTS, lanes), 0)
    one = jnp.ones((SEGMENTS, lanes), jnp.float32)
    zero = jnp.zeros((SEGMENTS, lanes), jnp.float32)
    omegas = [angular_of(f, freq_local, freq_total) for f in range(freq_local)]

    def velocity(t):
        return vel_ref[core, pl.ds(t, SEGMENTS, stride=steps), :]

    for t in range(steps):
        psi = PHASE * (1.0 / velocity(t) - 1.0 / 3.0)
        for f in range(freq_local):
            sin, cos = sin_cos(omegas[f] * psi)
            re = wave_ref[0, f, pl.ds(t, SEGMENTS, stride=steps), :]
            im = wave_ref[1, f, pl.ds(t, SEGMENTS, stride=steps), :]
            screened_ref[f, 0, t] = re * cos - im * sin
            screened_ref[f, 1, t] = re * sin + im * cos

    rows_ref[...] = jnp.zeros(rows_ref.shape, jnp.float32)
    for f in range(freq_local):
        wave = lambda t: (screened_ref[f, 0, t], screened_ref[f, 1, t])
        state = [[(one, zero), (zero, zero)], [(zero, zero), (one, zero)], [(zero, zero), (zero, zero)]]
        for t in range(steps):
            eps = inverse_kappa(velocity(t), omegas[f])
            g = source_terms(wave, t, steps, eps, rows)
            for i in range(3):
                w, d = state[i]
                d = sub(d, mul(eps, w))
                if i == 2:
                    d = add(d, g)
                state[i] = [add(w, d), d]
        (m00, m10), (m01, m11), (v0, v1) = state
        distance = 1
        while distance < SEGMENTS:
            b00, b01, b10, b11, bv0, bv1 = [
                (pltpu.roll(q[0], distance, 0), pltpu.roll(q[1], distance, 0))
                for q in (m00, m01, m10, m11, v0, v1)
            ]
            new = (
                add(mul(m00, b00), mul(m01, b10)),
                add(mul(m00, b01), mul(m01, b11)),
                add(mul(m10, b00), mul(m11, b10)),
                add(mul(m10, b01), mul(m11, b11)),
                add(add(mul(m00, bv0), mul(m01, bv1)), v0),
                add(add(mul(m10, bv0), mul(m11, bv1)), v1),
            )
            use = rows >= distance
            m00, m01, m10, m11, v0, v1 = [
                (jnp.where(use, n[0], q[0]), jnp.where(use, n[1], q[1]))
                for n, q in zip(new, (m00, m01, m10, m11, v0, v1))
            ]
            distance *= 2
        for i, q in enumerate((m00, m01, m10, m11, v0, v1)):
            scan_ref[f, 2 * i] = q[0]
            scan_ref[f, 2 * i + 1] = q[1]
        r = reciprocal(m01)
        b = mul(m11, r)
        fields = (r, mul(m00, r), b, mul(r, v0), sub(v1, mul(b, v0)))
        base = f * FIELDS * 2
        for i, q in enumerate(fields):
            for c in range(2):
                rows_ref[base + 2 * i + c : base + 2 * i + c + 1, :] = q[c][SEGMENTS - 1 :, :]
        for c in range(2):
            rows_ref[base + 10 + c : base + 11 + c, :] = screened_ref[f, c, 0][0:1, :]
            rows_ref[base + 12 + c : base + 13 + c, :] = screened_ref[f, c, steps - 1][SEGMENTS - 1 :, :]
    tail = freq_local * FIELDS * 2
    rows_ref[tail : tail + 1, :] = velocity(0)[0:1, :]
    rows_ref[tail + 1 : tail + 2, :] = velocity(steps - 1)[SEGMENTS - 1 :, :]
    whole = rows_ref[...]
    for s in range(message_ref.shape[0]):
        message_ref[s] = whole


def backward_kernel(freq_total, owner_ref, gathered_ref, screened_ref, scan_ref, vel_ref, out_ref, image_ref, pick_ref):
    freq_local, cells = out_ref.shape[1], out_ref.shape[2]
    steps = cells // SEGMENTS
    lanes = out_ref.shape[3]
    strips = gathered_ref.shape[0] // MESSAGE
    core = lax.rem(owner_ref[0], CC)
    strip = lax.axis_index("zl") * XX + lax.axis_index("x")
    rows = lax.broadcasted_iota(jnp.int32, (SEGMENTS, lanes), 0)
    places = lax.broadcasted_iota(jnp.int32, (strips, lanes), 0)
    omegas = [angular_of(f, freq_local, freq_total) for f in range(freq_local)]

    def field(i):
        return gathered_ref[pl.ds(i, strips, stride=MESSAGE), :]

    tail = freq_local * FIELDS * 2
    vel_head, vel_tail = field(tail), field(tail + 1)
    for f in range(freq_local):
        base = f * FIELDS * 2
        r, a, b, q0, q1, p_head, p_tail = [
            (field(base + 2 * i), field(base + 2 * i + 1)) for i in range(FIELDS)
        ]
        eps_head = inverse_kappa(vel_head, omegas[f])
        eps_tail = inverse_kappa(vel_tail, omegas[f])
        e = mul(scale(2.0 * BETA, eps_head), shift_pair(p_tail, 1, places))
        c = mul(scale(2.0 * BETA, eps_tail), shift_pair(p_head, -1, places))
        carry = add(q1, sub(c, mul(c, b)))
        inner = add(q0, mul(r, c))
        rhs = add(add(inner, e), shift_pair(carry, 1, places))
        b_below = shift_pair(b, 1, places)
        diag = add(a, (jnp.where(places == 0, 1.0, b_below[0]), b_below[1]))
        inv = neg(reciprocal(diag))
        low = mul(shift_pair(r, 1, places), inv)
        edge = places == strips - 1
        up = mul((jnp.where(edge, 0.0, r[0]), jnp.where(edge, 0.0, r[1])), inv)
        rhs = mul(rhs, inv)
        distance = 1
        while distance < strips:
            low_b, up_b, rhs_b = [shift_pair(q, distance, places) for q in (low, up, rhs)]
            low_a, up_a, rhs_a = [shift_pair(q, -distance, places) for q in (low, up, rhs)]
            pivot = add(mul(low, up_b), mul(up, low_a))
            inv = reciprocal((1.0 - pivot[0], -pivot[1]))
            rhs = mul(sub(rhs, add(mul(low, rhs_b), mul(up, rhs_a))), inv)
            if 2 * distance < strips:
                low, up = neg(mul(mul(low, low_b), inv)), neg(mul(mul(up, up_a), inv))
            distance *= 2
        slope = sub(mul(r, shift_pair(rhs, -1, places)), add(mul(a, rhs), inner))
        for i, q in enumerate((rhs[0], rhs[1], slope[0], slope[1])):
            pick_ref[4 * f + i] = q

    state = []
    for f in range(freq_local):
        w_in, d_in = [
            tuple(
                jnp.broadcast_to(pick_ref[4 * f + 2 * i + c, pl.ds(strip, 1), :], (SEGMENTS, lanes))
                for c in range(2)
            )
            for i in range(2)
        ]
        m00, m01, m10, m11, v0, v1 = [
            shift_pair((scan_ref[f, 2 * i], scan_ref[f, 2 * i + 1]), 1, rows) for i in range(6)
        ]
        first = rows == 0
        m00 = (jnp.where(first, 1.0, m00[0]), m00[1])
        m11 = (jnp.where(first, 1.0, m11[0]), m11[1])
        w = add(add(mul(m00, w_in), mul(m01, d_in)), v0)
        d = add(add(mul(m10, w_in), mul(m11, d_in)), v1)
        state.append((w, d))
    for t in range(steps):
        image = None
        vel = vel_ref[core, pl.ds(t, SEGMENTS, stride=steps), :]
        for f in range(freq_local):
            wave = lambda t: (screened_ref[f, 0, t], screened_ref[f, 1, t])
            w, d = state[f]
            out = sub(w, wave(t))
            out_ref[0, f, pl.ds(t, SEGMENTS, stride=steps), :] = out[0]
            out_ref[1, f, pl.ds(t, SEGMENTS, stride=steps), :] = out[1]
            image = out[0] if image is None else image + out[0]
            if t < steps - 1:
                eps = inverse_kappa(vel, omegas[f])
                d = add(sub(d, mul(eps, w)), source_terms(wave, t, steps, eps, rows))
                state[f] = (add(w, d), d)
        image_ref[pl.ds(t, SEGMENTS, stride=steps), :] = image


def tree(axes, index, count, source, value):
    place, core = source

    def pair(a, b):
        return ((a % count) * CC + core, (b % count) * CC + core)

    up = lax.ppermute(value, axes, [pair(place, place + 1)])
    far = lax.ppermute(up, axes, [pair(place + 1, place + 2)])
    down = lax.ppermute(value, axes, [pair(place, place - 1)])
    return jnp.where(index == place, value, up + far + down)


def spread(value, axis, count, place, core):
    index = lax.axis_index(axis)
    branches = [
        functools.partial(tree, (axis, "c"), index, count, (p, c)) for p in range(count) for c in range(CC)
    ]
    return lax.switch(place * CC + core, branches, value)


def strip_call(kernel, outs, scratch, smem_args, args):
    return pl.pallas_call(
        kernel,
        out_shape=outs,
        in_specs=[pl.BlockSpec(memory_space=pltpu.SMEM)] * smem_args
        + [pl.BlockSpec(memory_space=pltpu.VMEM)] * (len(args) - smem_args),
        out_specs=[pl.BlockSpec(memory_space=pltpu.VMEM)] * len(outs),
        scratch_shapes=scratch,
        compiler_params=pltpu.CompilerParams(vmem_limit_bytes=32 * 1024 * 1024),
    )(*args)


PAIRS_ONE = [(0, 1), (1, 0), (2, 3), (3, 2)]
PAIRS_TWO = [(1, 2), (2, 1), (3, 0), (0, 3)]


def shards(wavefield, velocity_bank, owner):
    freq_local, cells, lanes = wavefield.shape[1:]
    steps = cells // SEGMENTS
    freq_total = freq_local * ZH * YY * CC
    struct = lambda *shape: jax.ShapeDtypeStruct(shape, jnp.float32)
    own = owner[0]
    core = own % CC
    velocity = spread(velocity_bank[0], "zh", ZH, own // (YY * CC), core)
    velocity = spread(velocity, "y", YY, (own // CC) % YY, core)
    velocity = lax.all_gather(velocity, "c", axis=0)
    screened, scan, message = strip_call(
        functools.partial(forward_kernel, freq_total),
        [
            struct(freq_local, 2, steps, SEGMENTS, lanes),
            struct(freq_local, 12, SEGMENTS, lanes),
            struct(N_STRIPS, MESSAGE, lanes),
        ],
        [pltpu.VMEM((MESSAGE, lanes), jnp.float32)],
        1,
        (owner, wavefield, velocity),
    )
    gathered = lax.all_to_all(message, STRIPS, 0, 0, tiled=True)
    wave_out, partial = strip_call(
        functools.partial(backward_kernel, freq_total),
        [struct(2, freq_local, cells, lanes), struct(cells, lanes)],
        [pltpu.VMEM((4 * freq_local, N_STRIPS, lanes), jnp.float32)],
        1,
        (owner, gathered.reshape(N_STRIPS * MESSAGE, lanes), screened, scan, velocity),
    )
    group = YY * CC
    pieces = lax.all_to_all(partial.reshape(group, cells // group, lanes), ("y", "c"), 0, 0, tiled=True)
    total = jnp.sum(pieces, axis=0)
    total = total + lax.ppermute(total, "zh", PAIRS_ONE)
    total = total + lax.ppermute(total, "zh", PAIRS_TWO)
    total = total * (1.0 / math.sqrt(freq_total))
    image = lax.all_to_all(
        jnp.broadcast_to(total, (group,) + total.shape), ("y", "c"), 0, 0, tiled=True
    )
    return (wave_out, image.reshape(cells, lanes))


def solution(mesh):
    grid = Mesh(mesh.devices.reshape(ZH, YY, CC, ZL, XX), FREQ + STRIPS)
    return jax.shard_map(
        shards,
        mesh=grid,
        in_specs=(P(None, FREQ, STRIPS, None), P(FREQ, STRIPS, None), P()),
        out_specs=(P(None, FREQ, STRIPS, None), P(STRIPS, None)),
        check_vma=False,
    )
```

```python
import functools
import math

import jax
import jax.numpy as jnp
from jax import lax
from jax.experimental import pallas as pl
from jax.experimental.pallas import tpu as pltpu
from jax.sharding import Mesh, PartitionSpec as P

BETA = 1.0 / 6.0
GAIN = 30000.0
PHASE = 2.0

ZH, YY, CC, ZL, XX = 4, 4, 2, 4, 4
FREQ = ("zh", "y", "c")
STRIPS = ("zl", "x")
N_STRIPS = ZL * XX
SEGMENTS = 8
FIELDS = 7
MESSAGE = 32


def mul(a, b):
    return (a[0] * b[0] - a[1] * b[1], a[0] * b[1] + a[1] * b[0])


def add(a, b):
    return (a[0] + b[0], a[1] + b[1])


def sub(a, b):
    return (a[0] - b[0], a[1] - b[1])


def neg(a):
    return (-a[0], -a[1])


def scale(s, a):
    return (s * a[0], s * a[1])


def reciprocal(a):
    inverse = 1.0 / (a[0] * a[0] + a[1] * a[1])
    return (a[0] * inverse, -a[1] * inverse)


def sin_cos(angle):
    h = 0.5 * angle
    z = h * h
    s = 1.0 / 6227020800.0
    for k in (-1.0 / 39916800.0, 1.0 / 362880.0, -1.0 / 5040.0, 1.0 / 120.0, -1.0 / 6.0):
        s = s * z + k
    s = h + h * (z * s)
    c = 1.0 / 87178291200.0
    c = -c * z + 1.0 / 479001600.0
    for k in (-1.0 / 3628800.0, 1.0 / 40320.0, -1.0 / 720.0, 1.0 / 24.0, -0.5):
        c = c * z + k
    c = 1.0 + z * c
    return 2.0 * s * c, 1.0 - 2.0 * s * s


def inverse_kappa(velocity, angular):
    big = GAIN * velocity * (1.0 / angular)
    inverse = 1.0 / (BETA * BETA + big * big)
    return (BETA * inverse, big * inverse)


def angular_of(f, freq_local, freq_total):
    index = (lax.axis_index("zh") * YY + lax.axis_index("y")) * CC + lax.axis_index("c")
    index = index * freq_local + f
    return 1.0 + 3.0 * index.astype(jnp.float32) / freq_total


def shift_rows(x, distance, rows):
    count = x.shape[0]
    rolled = pltpu.roll(x, distance % count, 0)
    inside = rows >= distance if distance > 0 else rows < count + distance
    return jnp.where(inside, rolled, 0.0)


def shift_pair(a, distance, rows):
    return (shift_rows(a[0], distance, rows), shift_rows(a[1], distance, rows))


def source_terms(wave, t, steps, eps, rows):
    here = wave(t)
    prev = wave(t - 1) if t > 0 else shift_pair(wave(steps - 1), 1, rows)
    after = wave(t + 1) if t < steps - 1 else shift_pair(wave(0), -1, rows)
    lap = sub(add(prev, after), scale(2.0, here))
    return mul(scale(2.0, eps), add(here, scale(BETA, lap)))


def forward_kernel(freq_total, owner_ref, wave_ref, vel_ref, screened_ref, scan_ref, message_ref, rows_ref):
    freq_local, cells = wave_ref.shape[1], wave_ref.shape[2]
    steps = cells // SEGMENTS
    lanes = wave_ref.shape[3]
    core = 0
    rows = lax.broadcasted_iota(jnp.int32, (SEGMENTS, lanes), 0)
    one = jnp.ones((SEGMENTS, lanes), jnp.float32)
    zero = jnp.zeros((SEGMENTS, lanes), jnp.float32)
    omegas = [angular_of(f, freq_local, freq_total) for f in range(freq_local)]

    def velocity(t):
        return vel_ref[core, pl.ds(t, SEGMENTS, stride=steps), :]

    for t in range(steps):
        psi = PHASE * (1.0 / velocity(t) - 1.0 / 3.0)
        for f in range(freq_local):
            sin, cos = sin_cos(omegas[f] * psi)
            re = wave_ref[0, f, pl.ds(t, SEGMENTS, stride=steps), :]
            im = wave_ref[1, f, pl.ds(t, SEGMENTS, stride=steps), :]
            screened_ref[f, 0, t] = re * cos - im * sin
            screened_ref[f, 1, t] = re * sin + im * cos

    rows_ref[...] = jnp.zeros(rows_ref.shape, jnp.float32)
    for f in range(freq_local):
        wave = lambda t: (screened_ref[f, 0, t], screened_ref[f, 1, t])
        state = [[(one, zero), (zero, zero)], [(zero, zero), (one, zero)], [(zero, zero), (zero, zero)]]
        for t in range(steps):
            eps = inverse_kappa(velocity(t), omegas[f])
            g = source_terms(wave, t, steps, eps, rows)
            for i in range(3):
                w, d = state[i]
                d = sub(d, mul(eps, w))
                if i == 2:
                    d = add(d, g)
                state[i] = [add(w, d), d]
        (m00, m10), (m01, m11), (v0, v1) = state
        distance = 1
        while distance < SEGMENTS:
            b00, b01, b10, b11, bv0, bv1 = [
                (pltpu.roll(q[0], distance, 0), pltpu.roll(q[1], distance, 0))
                for q in (m00, m01, m10, m11, v0, v1)
            ]
            new = (
                add(mul(m00, b00), mul(m01, b10)),
                add(mul(m00, b01), mul(m01, b11)),
                add(mul(m10, b00), mul(m11, b10)),
                add(mul(m10, b01), mul(m11, b11)),
                add(add(mul(m00, bv0), mul(m01, bv1)), v0),
                add(add(mul(m10, bv0), mul(m11, bv1)), v1),
            )
            use = rows >= distance
            m00, m01, m10, m11, v0, v1 = [
                (jnp.where(use, n[0], q[0]), jnp.where(use, n[1], q[1]))
                for n, q in zip(new, (m00, m01, m10, m11, v0, v1))
            ]
            distance *= 2
        for i, q in enumerate((m00, m01, m10, m11, v0, v1)):
            scan_ref[f, 2 * i] = q[0]
            scan_ref[f, 2 * i + 1] = q[1]
        r = reciprocal(m01)
        b = mul(m11, r)
        fields = (r, mul(m00, r), b, mul(r, v0), sub(v1, mul(b, v0)))
        base = f * FIELDS * 2
        for i, q in enumerate(fields):
            for c in range(2):
                rows_ref[base + 2 * i + c : base + 2 * i + c + 1, :] = q[c][SEGMENTS - 1 :, :]
        for c in range(2):
            rows_ref[base + 10 + c : base + 11 + c, :] = screened_ref[f, c, 0][0:1, :]
            rows_ref[base + 12 + c : base + 13 + c, :] = screened_ref[f, c, steps - 1][SEGMENTS - 1 :, :]
    tail = freq_local * FIELDS * 2
    rows_ref[tail : tail + 1, :] = velocity(0)[0:1, :]
    rows_ref[tail + 1 : tail + 2, :] = velocity(steps - 1)[SEGMENTS - 1 :, :]
    whole = rows_ref[...]
    for s in range(message_ref.shape[0]):
        message_ref[s] = whole


def backward_kernel(freq_total, owner_ref, gathered_ref, screened_ref, scan_ref, vel_ref, out_ref, image_ref, pick_ref):
    freq_local, cells = out_ref.shape[1], out_ref.shape[2]
    steps = cells // SEGMENTS
    lanes = out_ref.shape[3]
    strips = gathered_ref.shape[0] // MESSAGE
    core = 0
    strip = lax.axis_index("zl") * XX + lax.axis_index("x")
    rows = lax.broadcasted_iota(jnp.int32, (SEGMENTS, lanes), 0)
    places = lax.broadcasted_iota(jnp.int32, (strips, lanes), 0)
    omegas = [angular_of(f, freq_local, freq_total) for f in range(freq_local)]

    def field(i):
        return gathered_ref[pl.ds(i, strips, stride=MESSAGE), :]

    tail = freq_local * FIELDS * 2
    vel_head, vel_tail = field(tail), field(tail + 1)
    for f in range(freq_local):
        base = f * FIELDS * 2
        r, a, b, q0, q1, p_head, p_tail = [
            (field(base + 2 * i), field(base + 2 * i + 1)) for i in range(FIELDS)
        ]
        eps_head = inverse_kappa(vel_head, omegas[f])
        eps_tail = inverse_kappa(vel_tail, omegas[f])
        e = mul(scale(2.0 * BETA, eps_head), shift_pair(p_tail, 1, places))
        c = mul(scale(2.0 * BETA, eps_tail), shift_pair(p_head, -1, places))
        carry = add(q1, sub(c, mul(c, b)))
        inner = add(q0, mul(r, c))
        rhs = add(add(inner, e), shift_pair(carry, 1, places))
        b_below = shift_pair(b, 1, places)
        diag = add(a, (jnp.where(places == 0, 1.0, b_below[0]), b_below[1]))
        inv = neg(reciprocal(diag))
        low = mul(shift_pair(r, 1, places), inv)
        edge = places == strips - 1
        up = mul((jnp.where(edge, 0.0, r[0]), jnp.where(edge, 0.0, r[1])), inv)
        rhs = mul(rhs, inv)
        distance = 1
        while distance < strips:
            low_b, up_b, rhs_b = [shift_pair(q, distance, places) for q in (low, up, rhs)]
            low_a, up_a, rhs_a = [shift_pair(q, -distance, places) for q in (low, up, rhs)]
            pivot = add(mul(low, up_b), mul(up, low_a))
            inv = reciprocal((1.0 - pivot[0], -pivot[1]))
            rhs = mul(sub(rhs, add(mul(low, rhs_b), mul(up, rhs_a))), inv)
            if 2 * distance < strips:
                low, up = neg(mul(mul(low, low_b), inv)), neg(mul(mul(up, up_a), inv))
            distance *= 2
        slope = sub(mul(r, shift_pair(rhs, -1, places)), add(mul(a, rhs), inner))
        for i, q in enumerate((rhs[0], rhs[1], slope[0], slope[1])):
            pick_ref[4 * f + i] = q

    state = []
    for f in range(freq_local):
        w_in, d_in = [
            tuple(
                jnp.broadcast_to(pick_ref[4 * f + 2 * i + c, pl.ds(strip, 1), :], (SEGMENTS, lanes))
                for c in range(2)
            )
            for i in range(2)
        ]
        m00, m01, m10, m11, v0, v1 = [
            shift_pair((scan_ref[f, 2 * i], scan_ref[f, 2 * i + 1]), 1, rows) for i in range(6)
        ]
        first = rows == 0
        m00 = (jnp.where(first, 1.0, m00[0]), m00[1])
        m11 = (jnp.where(first, 1.0, m11[0]), m11[1])
        w = add(add(mul(m00, w_in), mul(m01, d_in)), v0)
        d = add(add(mul(m10, w_in), mul(m11, d_in)), v1)
        state.append((w, d))
    for t in range(steps):
        image = None
        vel = vel_ref[core, pl.ds(t, SEGMENTS, stride=steps), :]
        for f in range(freq_local):
            wave = lambda t: (screened_ref[f, 0, t], screened_ref[f, 1, t])
            w, d = state[f]
            out = sub(w, wave(t))
            out_ref[0, f, pl.ds(t, SEGMENTS, stride=steps), :] = out[0]
            out_ref[1, f, pl.ds(t, SEGMENTS, stride=steps), :] = out[1]
            image = out[0] if image is None else image + out[0]
            if t < steps - 1:
                eps = inverse_kappa(vel, omegas[f])
                d = add(sub(d, mul(eps, w)), source_terms(wave, t, steps, eps, rows))
                state[f] = (add(w, d), d)
        image_ref[pl.ds(t, SEGMENTS, stride=steps), :] = image


def tree(axes, index, count, source, value):
    place, core = source

    def pair(a, b):
        return ((a % count) * CC + core, (b % count) * CC + core)

    up = lax.ppermute(value, axes, [pair(place, place + 1)])
    far = lax.ppermute(up, axes, [pair(place + 1, place + 2)])
    down = lax.ppermute(value, axes, [pair(place, place - 1)])
    return jnp.where(index == place, value, up + far + down)


def spread(value, axis, count, place, core):
    index = lax.axis_index(axis)
    branches = [
        functools.partial(tree, (axis, "c"), index, count, (p, c)) for p in range(count) for c in range(CC)
    ]
    return lax.switch(place * CC + core, branches, value)


def spread_plain(value, axis, count, place):
    index = lax.axis_index(axis)

    def branch(p):
        def run(x):
            at = lambda i: i % count
            far = lax.ppermute(x, axis, [(p, at(p + 2))])
            up = lax.ppermute(x, axis, [(p, at(p + 1))])
            down = lax.ppermute(x, axis, [(p, at(p - 1))])
            return jnp.where(index == p, x, up + far + down)

        return run

    return lax.switch(place, [branch(p) for p in range(count)], value)


def strip_call(kernel, outs, scratch, smem_args, args):
    return pl.pallas_call(
        kernel,
        out_shape=outs,
        in_specs=[pl.BlockSpec(memory_space=pltpu.SMEM)] * smem_args
        + [pl.BlockSpec(memory_space=pltpu.VMEM)] * (len(args) - smem_args),
        out_specs=[pl.BlockSpec(memory_space=pltpu.VMEM)] * len(outs),
        scratch_shapes=scratch,
        compiler_params=pltpu.CompilerParams(vmem_limit_bytes=32 * 1024 * 1024),
    )(*args)


PAIRS_ONE = [(0, 1), (1, 0), (2, 3), (3, 2)]
PAIRS_TWO = [(1, 2), (2, 1), (3, 0), (0, 3)]


def shards(wavefield, velocity_bank, owner):
    freq_local, cells, lanes = wavefield.shape[1:]
    steps = cells // SEGMENTS
    freq_total = freq_local * ZH * YY * CC
    struct = lambda *shape: jax.ShapeDtypeStruct(shape, jnp.float32)
    own = owner[0]
    core = own % CC
    group, rows = YY * CC, cells // (YY * CC)
    home = own // group

    def scatter(slab):
        parts = lax.all_to_all(slab.reshape(group, rows, lanes), ("y", "c"), 0, 0, tiled=True)
        return lax.dynamic_index_in_dim(parts, own % group, 0, keepdims=False)

    piece = lax.cond(
        lax.axis_index("zh") == home, scatter, lambda slab: slab[:rows], velocity_bank[0]
    )
    piece = spread_plain(piece, "zh", ZH, own // group)
    velocity = lax.all_to_all(
        jnp.broadcast_to(piece, (group,) + piece.shape), ("y", "c"), 0, 0, tiled=True
    ).reshape(1, cells, lanes)
    screened, scan, message = strip_call(
        functools.partial(forward_kernel, freq_total),
        [
            struct(freq_local, 2, steps, SEGMENTS, lanes),
            struct(freq_local, 12, SEGMENTS, lanes),
            struct(N_STRIPS, MESSAGE, lanes),
        ],
        [pltpu.VMEM((MESSAGE, lanes), jnp.float32)],
        1,
        (owner, wavefield, velocity),
    )
    gathered = lax.all_to_all(message, STRIPS, 0, 0, tiled=True)
    wave_out, partial = strip_call(
        functools.partial(backward_kernel, freq_total),
        [struct(2, freq_local, cells, lanes), struct(cells, lanes)],
        [pltpu.VMEM((4 * freq_local, N_STRIPS, lanes), jnp.float32)],
        1,
        (owner, gathered.reshape(N_STRIPS * MESSAGE, lanes), screened, scan, velocity),
    )
    group = YY * CC
    pieces = lax.all_to_all(partial.reshape(group, cells // group, lanes), ("y", "c"), 0, 0, tiled=True)
    total = jnp.sum(pieces, axis=0)
    total = total + lax.ppermute(total, "zh", PAIRS_ONE)
    total = total + lax.ppermute(total, "zh", PAIRS_TWO)
    total = total * (1.0 / math.sqrt(freq_total))
    image = lax.all_to_all(
        jnp.broadcast_to(total, (group,) + total.shape), ("y", "c"), 0, 0, tiled=True
    )
    return (wave_out, image.reshape(cells, lanes))


def solution(mesh):
    grid = Mesh(mesh.devices.reshape(ZH, YY, CC, ZL, XX), FREQ + STRIPS)
    return jax.shard_map(
        shards,
        mesh=grid,
        in_specs=(P(None, FREQ, STRIPS, None), P(FREQ, STRIPS, None), P()),
        out_specs=(P(None, FREQ, STRIPS, None), P(STRIPS, None)),
        check_vma=False,
    )
```

```python
import functools
import math

import jax
import jax.numpy as jnp
from jax import lax
from jax.experimental import pallas as pl
from jax.experimental.pallas import tpu as pltpu
from jax.sharding import Mesh, PartitionSpec as P

BETA = 1.0 / 6.0
GAIN = 30000.0
PHASE = 2.0

ZH, YY, CC, ZL, XX = 4, 4, 2, 4, 4
FREQ = ("zh", "y", "c")
STRIPS = ("zl", "x")
N_STRIPS = ZL * XX
SEGMENTS = 8
FIELDS = 7
MESSAGE = 32


def mul(a, b):
    return (a[0] * b[0] - a[1] * b[1], a[0] * b[1] + a[1] * b[0])


def add(a, b):
    return (a[0] + b[0], a[1] + b[1])


def sub(a, b):
    return (a[0] - b[0], a[1] - b[1])


def neg(a):
    return (-a[0], -a[1])


def scale(s, a):
    return (s * a[0], s * a[1])


def reciprocal(a):
    inverse = 1.0 / (a[0] * a[0] + a[1] * a[1])
    return (a[0] * inverse, -a[1] * inverse)


def sin_cos(angle):
    h = 0.5 * angle
    z = h * h
    s = 1.0 / 6227020800.0
    for k in (-1.0 / 39916800.0, 1.0 / 362880.0, -1.0 / 5040.0, 1.0 / 120.0, -1.0 / 6.0):
        s = s * z + k
    s = h + h * (z * s)
    c = 1.0 / 87178291200.0
    c = -c * z + 1.0 / 479001600.0
    for k in (-1.0 / 3628800.0, 1.0 / 40320.0, -1.0 / 720.0, 1.0 / 24.0, -0.5):
        c = c * z + k
    c = 1.0 + z * c
    return 2.0 * s * c, 1.0 - 2.0 * s * s


def inverse_kappa(velocity, angular):
    big = GAIN * velocity * (1.0 / angular)
    inverse = 1.0 / (BETA * BETA + big * big)
    return (BETA * inverse, big * inverse)


def angular_of(f, freq_local, freq_total):
    index = (lax.axis_index("zh") * YY + lax.axis_index("y")) * CC + lax.axis_index("c")
    index = index * freq_local + f
    return 1.0 + 3.0 * index.astype(jnp.float32) / freq_total


def shift_rows(x, distance, rows):
    count = x.shape[0]
    rolled = pltpu.roll(x, distance % count, 0)
    inside = rows >= distance if distance > 0 else rows < count + distance
    return jnp.where(inside, rolled, 0.0)


def shift_pair(a, distance, rows):
    return (shift_rows(a[0], distance, rows), shift_rows(a[1], distance, rows))


def source_terms(wave, t, steps, eps, rows):
    here = wave(t)
    prev = wave(t - 1) if t > 0 else shift_pair(wave(steps - 1), 1, rows)
    after = wave(t + 1) if t < steps - 1 else shift_pair(wave(0), -1, rows)
    lap = sub(add(prev, after), scale(2.0, here))
    return mul(scale(2.0, eps), add(here, scale(BETA, lap)))


def forward_kernel(freq_total, owner_ref, wave_ref, vel_ref, screened_ref, scan_ref, message_ref, rows_ref):
    freq_local, cells = wave_ref.shape[1], wave_ref.shape[2]
    steps = cells // SEGMENTS
    lanes = wave_ref.shape[3]
    core = 0
    rows = lax.broadcasted_iota(jnp.int32, (SEGMENTS, lanes), 0)
    one = jnp.ones((SEGMENTS, lanes), jnp.float32)
    zero = jnp.zeros((SEGMENTS, lanes), jnp.float32)
    omegas = [angular_of(f, freq_local, freq_total) for f in range(freq_local)]

    def velocity(t):
        return vel_ref[core, pl.ds(t, SEGMENTS, stride=steps), :]

    for t in range(steps):
        psi = PHASE * (1.0 / velocity(t) - 1.0 / 3.0)
        for f in range(freq_local):
            sin, cos = sin_cos(omegas[f] * psi)
            re = wave_ref[0, f, pl.ds(t, SEGMENTS, stride=steps), :]
            im = wave_ref[1, f, pl.ds(t, SEGMENTS, stride=steps), :]
            screened_ref[f, 0, t] = re * cos - im * sin
            screened_ref[f, 1, t] = re * sin + im * cos

    rows_ref[...] = jnp.zeros(rows_ref.shape, jnp.float32)
    for f in range(freq_local):
        wave = lambda t: (screened_ref[f, 0, t], screened_ref[f, 1, t])
        state = [[(one, zero), (zero, zero)], [(zero, zero), (one, zero)], [(zero, zero), (zero, zero)]]
        for t in range(steps):
            eps = inverse_kappa(velocity(t), omegas[f])
            g = source_terms(wave, t, steps, eps, rows)
            for i in range(3):
                w, d = state[i]
                d = sub(d, mul(eps, w))
                if i == 2:
                    d = add(d, g)
                state[i] = [add(w, d), d]
        (m00, m10), (m01, m11), (v0, v1) = state
        distance = 1
        while distance < SEGMENTS:
            b00, b01, b10, b11, bv0, bv1 = [
                (pltpu.roll(q[0], distance, 0), pltpu.roll(q[1], distance, 0))
                for q in (m00, m01, m10, m11, v0, v1)
            ]
            new = (
                add(mul(m00, b00), mul(m01, b10)),
                add(mul(m00, b01), mul(m01, b11)),
                add(mul(m10, b00), mul(m11, b10)),
                add(mul(m10, b01), mul(m11, b11)),
                add(add(mul(m00, bv0), mul(m01, bv1)), v0),
                add(add(mul(m10, bv0), mul(m11, bv1)), v1),
            )
            use = rows >= distance
            m00, m01, m10, m11, v0, v1 = [
                (jnp.where(use, n[0], q[0]), jnp.where(use, n[1], q[1]))
                for n, q in zip(new, (m00, m01, m10, m11, v0, v1))
            ]
            distance *= 2
        for i, q in enumerate((m00, m01, m10, m11, v0, v1)):
            scan_ref[f, 2 * i] = q[0]
            scan_ref[f, 2 * i + 1] = q[1]
        r = reciprocal(m01)
        b = mul(m11, r)
        fields = (r, mul(m00, r), b, mul(r, v0), sub(v1, mul(b, v0)))
        base = f * FIELDS * 2
        for i, q in enumerate(fields):
            for c in range(2):
                rows_ref[base + 2 * i + c : base + 2 * i + c + 1, :] = q[c][SEGMENTS - 1 :, :]
        for c in range(2):
            rows_ref[base + 10 + c : base + 11 + c, :] = screened_ref[f, c, 0][0:1, :]
            rows_ref[base + 12 + c : base + 13 + c, :] = screened_ref[f, c, steps - 1][SEGMENTS - 1 :, :]
    tail = freq_local * FIELDS * 2
    rows_ref[tail : tail + 1, :] = velocity(0)[0:1, :]
    rows_ref[tail + 1 : tail + 2, :] = velocity(steps - 1)[SEGMENTS - 1 :, :]
    whole = rows_ref[...]
    for s in range(message_ref.shape[0]):
        message_ref[s] = whole


def backward_kernel(freq_total, owner_ref, gathered_ref, screened_ref, scan_ref, vel_ref, out_ref, image_ref, pick_ref):
    freq_local, cells = out_ref.shape[1], out_ref.shape[2]
    steps = cells // SEGMENTS
    lanes = out_ref.shape[3]
    strips = gathered_ref.shape[0] // MESSAGE
    core = 0
    strip = lax.axis_index("zl") * XX + lax.axis_index("x")
    rows = lax.broadcasted_iota(jnp.int32, (SEGMENTS, lanes), 0)
    places = lax.broadcasted_iota(jnp.int32, (strips, lanes), 0)
    omegas = [angular_of(f, freq_local, freq_total) for f in range(freq_local)]

    def field(i):
        return gathered_ref[pl.ds(i, strips, stride=MESSAGE), :]

    tail = freq_local * FIELDS * 2
    vel_head, vel_tail = field(tail), field(tail + 1)
    for f in range(freq_local):
        base = f * FIELDS * 2
        r, a, b, q0, q1, p_head, p_tail = [
            (field(base + 2 * i), field(base + 2 * i + 1)) for i in range(FIELDS)
        ]
        eps_head = inverse_kappa(vel_head, omegas[f])
        eps_tail = inverse_kappa(vel_tail, omegas[f])
        e = mul(scale(2.0 * BETA, eps_head), shift_pair(p_tail, 1, places))
        c = mul(scale(2.0 * BETA, eps_tail), shift_pair(p_head, -1, places))
        carry = add(q1, sub(c, mul(c, b)))
        inner = add(q0, mul(r, c))
        rhs = add(add(inner, e), shift_pair(carry, 1, places))
        b_below = shift_pair(b, 1, places)
        diag = add(a, (jnp.where(places == 0, 1.0, b_below[0]), b_below[1]))
        inv = neg(reciprocal(diag))
        low = mul(shift_pair(r, 1, places), inv)
        edge = places == strips - 1
        up = mul((jnp.where(edge, 0.0, r[0]), jnp.where(edge, 0.0, r[1])), inv)
        rhs = mul(rhs, inv)
        distance = 1
        while distance < strips:
            low_b, up_b, rhs_b = [shift_pair(q, distance, places) for q in (low, up, rhs)]
            low_a, up_a, rhs_a = [shift_pair(q, -distance, places) for q in (low, up, rhs)]
            pivot = add(mul(low, up_b), mul(up, low_a))
            inv = reciprocal((1.0 - pivot[0], -pivot[1]))
            rhs = mul(sub(rhs, add(mul(low, rhs_b), mul(up, rhs_a))), inv)
            if 2 * distance < strips:
                low, up = neg(mul(mul(low, low_b), inv)), neg(mul(mul(up, up_a), inv))
            distance *= 2
        slope = sub(mul(r, shift_pair(rhs, -1, places)), add(mul(a, rhs), inner))
        for i, q in enumerate((rhs[0], rhs[1], slope[0], slope[1])):
            pick_ref[4 * f + i] = q

    state = []
    for f in range(freq_local):
        w_in, d_in = [
            tuple(
                jnp.broadcast_to(pick_ref[4 * f + 2 * i + c, pl.ds(strip, 1), :], (SEGMENTS, lanes))
                for c in range(2)
            )
            for i in range(2)
        ]
        m00, m01, m10, m11, v0, v1 = [
            shift_pair((scan_ref[f, 2 * i], scan_ref[f, 2 * i + 1]), 1, rows) for i in range(6)
        ]
        first = rows == 0
        m00 = (jnp.where(first, 1.0, m00[0]), m00[1])
        m11 = (jnp.where(first, 1.0, m11[0]), m11[1])
        w = add(add(mul(m00, w_in), mul(m01, d_in)), v0)
        d = add(add(mul(m10, w_in), mul(m11, d_in)), v1)
        state.append((w, d))
    for t in range(steps):
        image = None
        vel = vel_ref[core, pl.ds(t, SEGMENTS, stride=steps), :]
        for f in range(freq_local):
            wave = lambda t: (screened_ref[f, 0, t], screened_ref[f, 1, t])
            w, d = state[f]
            out = sub(w, wave(t))
            out_ref[0, f, pl.ds(t, SEGMENTS, stride=steps), :] = out[0]
            out_ref[1, f, pl.ds(t, SEGMENTS, stride=steps), :] = out[1]
            image = out[0] if image is None else image + out[0]
            if t < steps - 1:
                eps = inverse_kappa(vel, omegas[f])
                d = add(sub(d, mul(eps, w)), source_terms(wave, t, steps, eps, rows))
                state[f] = (add(w, d), d)
        image_ref[pl.ds(t, SEGMENTS, stride=steps), :] = image


def spread(value, axis, count, place):
    index = lax.axis_index(axis)

    def branch(p):
        def run(x):
            at = lambda i: i % count
            far = lax.ppermute(x, axis, [(p, at(p + 2))])
            up = lax.ppermute(x, axis, [(p, at(p + 1))])
            down = lax.ppermute(x, axis, [(p, at(p - 1))])
            return jnp.where(index == p, x, up + far + down)

        return run

    return lax.switch(place, [branch(p) for p in range(count)], value)


def strip_call(kernel, outs, scratch, smem_args, args):
    return pl.pallas_call(
        kernel,
        out_shape=outs,
        in_specs=[pl.BlockSpec(memory_space=pltpu.SMEM)] * smem_args
        + [pl.BlockSpec(memory_space=pltpu.VMEM)] * (len(args) - smem_args),
        out_specs=[pl.BlockSpec(memory_space=pltpu.VMEM)] * len(outs),
        scratch_shapes=scratch,
        compiler_params=pltpu.CompilerParams(vmem_limit_bytes=32 * 1024 * 1024),
    )(*args)


PAIRS_ONE = [(0, 1), (1, 0), (2, 3), (3, 2)]
PAIRS_TWO = [(1, 2), (2, 1), (3, 0), (0, 3)]


def shards(wavefield, velocity_bank, owner):
    freq_local, cells, lanes = wavefield.shape[1:]
    steps = cells // SEGMENTS
    freq_total = freq_local * ZH * YY * CC
    struct = lambda *shape: jax.ShapeDtypeStruct(shape, jnp.float32)
    own = owner[0]
    core = own % CC
    group, half = YY * CC, cells // CC
    home, line = own // group, (own // CC) % YY
    at_home = lax.axis_index("zh") == home

    def share(slab):
        both = lax.all_gather(slab, "c", axis=0)
        return lax.dynamic_slice(both, (core, lax.axis_index("c") * half, 0), (1, half, lanes))[0]

    piece = lax.cond(
        at_home & (lax.axis_index("y") == line), share, lambda slab: slab[:half], velocity_bank[0]
    )
    piece = lax.cond(at_home, lambda x: spread(x, "y", YY, line), lambda x: x, piece)
    piece = spread(piece, "zh", ZH, home)
    velocity = lax.all_gather(piece, "c", axis=0, tiled=True).reshape(1, cells, lanes)
    screened, scan, message = strip_call(
        functools.partial(forward_kernel, freq_total),
        [
            struct(freq_local, 2, steps, SEGMENTS, lanes),
            struct(freq_local, 12, SEGMENTS, lanes),
            struct(N_STRIPS, MESSAGE, lanes),
        ],
        [pltpu.VMEM((MESSAGE, lanes), jnp.float32)],
        1,
        (owner, wavefield, velocity),
    )
    gathered = lax.all_to_all(message, STRIPS, 0, 0, tiled=True)
    wave_out, partial = strip_call(
        functools.partial(backward_kernel, freq_total),
        [struct(2, freq_local, cells, lanes), struct(cells, lanes)],
        [pltpu.VMEM((4 * freq_local, N_STRIPS, lanes), jnp.float32)],
        1,
        (owner, gathered.reshape(N_STRIPS * MESSAGE, lanes), screened, scan, velocity),
    )
    both = lax.all_gather(partial, "c", axis=0)
    begin = lax.axis_index("c") * half
    total = jnp.sum(lax.dynamic_slice(both, (0, begin, 0), (CC, half, lanes)), axis=0)
    total = jnp.sum(
        lax.all_to_all(jnp.broadcast_to(total, (YY, half, lanes)), "y", 0, 0, tiled=True), axis=0
    )
    total = total + lax.ppermute(total, "zh", PAIRS_ONE)
    total = total + lax.ppermute(total, "zh", PAIRS_TWO)
    total = total * (1.0 / math.sqrt(freq_total))
    image = lax.all_gather(total, "c", axis=0, tiled=True)
    return (wave_out, image.reshape(cells, lanes))


def solution(mesh):
    grid = Mesh(mesh.devices.reshape(ZH, YY, CC, ZL, XX), FREQ + STRIPS)
    return jax.shard_map(
        shards,
        mesh=grid,
        in_specs=(P(None, FREQ, STRIPS, None), P(FREQ, STRIPS, None), P()),
        out_specs=(P(None, FREQ, STRIPS, None), P(STRIPS, None)),
        check_vma=False,
    )
```

```python
import functools
import math

import jax
import jax.numpy as jnp
from jax import lax
from jax.experimental import pallas as pl
from jax.experimental.pallas import tpu as pltpu
from jax.sharding import Mesh, PartitionSpec as P

BETA = 1.0 / 6.0
GAIN = 30000.0
PHASE = 2.0

ZH, YY, CC, ZL, XX = 4, 4, 2, 4, 4
FREQ = ("zh", "y", "c")
STRIPS = ("zl", "x")
N_STRIPS = ZL * XX
SEGMENTS = 8
FIELDS = 7
MESSAGE = 32


def mul(a, b):
    return (a[0] * b[0] - a[1] * b[1], a[0] * b[1] + a[1] * b[0])


def add(a, b):
    return (a[0] + b[0], a[1] + b[1])


def sub(a, b):
    return (a[0] - b[0], a[1] - b[1])


def neg(a):
    return (-a[0], -a[1])


def scale(s, a):
    return (s * a[0], s * a[1])


def reciprocal(a):
    inverse = 1.0 / (a[0] * a[0] + a[1] * a[1])
    return (a[0] * inverse, -a[1] * inverse)


def sin_cos(angle):
    h = 0.5 * angle
    z = h * h
    s = 1.0 / 6227020800.0
    for k in (-1.0 / 39916800.0, 1.0 / 362880.0, -1.0 / 5040.0, 1.0 / 120.0, -1.0 / 6.0):
        s = s * z + k
    s = h + h * (z * s)
    c = 1.0 / 87178291200.0
    c = -c * z + 1.0 / 479001600.0
    for k in (-1.0 / 3628800.0, 1.0 / 40320.0, -1.0 / 720.0, 1.0 / 24.0, -0.5):
        c = c * z + k
    c = 1.0 + z * c
    return 2.0 * s * c, 1.0 - 2.0 * s * s


def inverse_kappa(velocity, angular):
    big = GAIN * velocity * (1.0 / angular)
    inverse = 1.0 / (BETA * BETA + big * big)
    return (BETA * inverse, big * inverse)


def angular_of(f, freq_local, freq_total):
    index = (lax.axis_index("zh") * YY + lax.axis_index("y")) * CC + lax.axis_index("c")
    index = index * freq_local + f
    return 1.0 + 3.0 * index.astype(jnp.float32) / freq_total


def shift_rows(x, distance, rows):
    count = x.shape[0]
    rolled = pltpu.roll(x, distance % count, 0)
    inside = rows >= distance if distance > 0 else rows < count + distance
    return jnp.where(inside, rolled, 0.0)


def shift_pair(a, distance, rows):
    return (shift_rows(a[0], distance, rows), shift_rows(a[1], distance, rows))


def source_terms(wave, t, steps, eps, rows):
    here = wave(t)
    prev = wave(t - 1) if t > 0 else shift_pair(wave(steps - 1), 1, rows)
    after = wave(t + 1) if t < steps - 1 else shift_pair(wave(0), -1, rows)
    lap = sub(add(prev, after), scale(2.0, here))
    return mul(scale(2.0, eps), add(here, scale(BETA, lap)))


def forward_kernel(freq_total, owner_ref, wave_ref, vel_ref, screened_ref, scan_ref, message_ref):
    freq_local, cells = wave_ref.shape[1], wave_ref.shape[2]
    steps = cells // SEGMENTS
    lanes = wave_ref.shape[3]
    core = 0
    rows = lax.broadcasted_iota(jnp.int32, (SEGMENTS, lanes), 0)
    one = jnp.ones((SEGMENTS, lanes), jnp.float32)
    zero = jnp.zeros((SEGMENTS, lanes), jnp.float32)
    omegas = [angular_of(f, freq_local, freq_total) for f in range(freq_local)]

    def velocity(t):
        return vel_ref[core, pl.ds(t, SEGMENTS, stride=steps), :]

    for t in range(steps):
        psi = PHASE * (1.0 / velocity(t) - 1.0 / 3.0)
        for f in range(freq_local):
            sin, cos = sin_cos(omegas[f] * psi)
            re = wave_ref[0, f, pl.ds(t, SEGMENTS, stride=steps), :]
            im = wave_ref[1, f, pl.ds(t, SEGMENTS, stride=steps), :]
            screened_ref[f, 0, t] = re * cos - im * sin
            screened_ref[f, 1, t] = re * sin + im * cos

    message_ref[...] = jnp.zeros(message_ref.shape, jnp.float32)
    for f in range(freq_local):
        wave = lambda t: (screened_ref[f, 0, t], screened_ref[f, 1, t])
        state = [[(one, zero), (zero, zero)], [(zero, zero), (one, zero)], [(zero, zero), (zero, zero)]]
        for t in range(steps):
            eps = inverse_kappa(velocity(t), omegas[f])
            g = source_terms(wave, t, steps, eps, rows)
            for i in range(3):
                w, d = state[i]
                d = sub(d, mul(eps, w))
                if i == 2:
                    d = add(d, g)
                state[i] = [add(w, d), d]
        (m00, m10), (m01, m11), (v0, v1) = state
        distance = 1
        while distance < SEGMENTS:
            b00, b01, b10, b11, bv0, bv1 = [
                (pltpu.roll(q[0], distance, 0), pltpu.roll(q[1], distance, 0))
                for q in (m00, m01, m10, m11, v0, v1)
            ]
            new = (
                add(mul(m00, b00), mul(m01, b10)),
                add(mul(m00, b01), mul(m01, b11)),
                add(mul(m10, b00), mul(m11, b10)),
                add(mul(m10, b01), mul(m11, b11)),
                add(add(mul(m00, bv0), mul(m01, bv1)), v0),
                add(add(mul(m10, bv0), mul(m11, bv1)), v1),
            )
            use = rows >= distance
            m00, m01, m10, m11, v0, v1 = [
                (jnp.where(use, n[0], q[0]), jnp.where(use, n[1], q[1]))
                for n, q in zip(new, (m00, m01, m10, m11, v0, v1))
            ]
            distance *= 2
        for i, q in enumerate((m00, m01, m10, m11, v0, v1)):
            scan_ref[f, 2 * i] = q[0]
            scan_ref[f, 2 * i + 1] = q[1]
        r = reciprocal(m01)
        b = mul(m11, r)
        fields = (r, mul(m00, r), b, mul(r, v0), sub(v1, mul(b, v0)))
        base = f * FIELDS * 2
        for i, q in enumerate(fields):
            for c in range(2):
                message_ref[base + 2 * i + c : base + 2 * i + c + 1, :] = q[c][SEGMENTS - 1 :, :]
        for c in range(2):
            message_ref[base + 10 + c : base + 11 + c, :] = screened_ref[f, c, 0][0:1, :]
            message_ref[base + 12 + c : base + 13 + c, :] = screened_ref[f, c, steps - 1][SEGMENTS - 1 :, :]
    tail = freq_local * FIELDS * 2
    message_ref[tail : tail + 1, :] = velocity(0)[0:1, :]
    message_ref[tail + 1 : tail + 2, :] = velocity(steps - 1)[SEGMENTS - 1 :, :]


def backward_kernel(freq_total, owner_ref, gathered_ref, screened_ref, scan_ref, vel_ref, out_ref, image_ref, pick_ref):
    freq_local, steps, _, lanes = out_ref.shape[1:]
    strips = gathered_ref.shape[0] // MESSAGE
    core = 0
    strip = lax.axis_index("zl") * XX + lax.axis_index("x")
    rows = lax.broadcasted_iota(jnp.int32, (SEGMENTS, lanes), 0)
    places = lax.broadcasted_iota(jnp.int32, (strips, lanes), 0)
    omegas = [angular_of(f, freq_local, freq_total) for f in range(freq_local)]

    def field(i):
        return gathered_ref[pl.ds(i, strips, stride=MESSAGE), :]

    tail = freq_local * FIELDS * 2
    vel_head, vel_tail = field(tail), field(tail + 1)
    for f in range(freq_local):
        base = f * FIELDS * 2
        r, a, b, q0, q1, p_head, p_tail = [
            (field(base + 2 * i), field(base + 2 * i + 1)) for i in range(FIELDS)
        ]
        eps_head = inverse_kappa(vel_head, omegas[f])
        eps_tail = inverse_kappa(vel_tail, omegas[f])
        e = mul(scale(2.0 * BETA, eps_head), shift_pair(p_tail, 1, places))
        c = mul(scale(2.0 * BETA, eps_tail), shift_pair(p_head, -1, places))
        carry = add(q1, sub(c, mul(c, b)))
        inner = add(q0, mul(r, c))
        rhs = add(add(inner, e), shift_pair(carry, 1, places))
        b_below = shift_pair(b, 1, places)
        diag = add(a, (jnp.where(places == 0, 1.0, b_below[0]), b_below[1]))
        inv = neg(reciprocal(diag))
        low = mul(shift_pair(r, 1, places), inv)
        edge = places == strips - 1
        up = mul((jnp.where(edge, 0.0, r[0]), jnp.where(edge, 0.0, r[1])), inv)
        rhs = mul(rhs, inv)
        distance = 1
        while distance < strips:
            low_b, up_b, rhs_b = [shift_pair(q, distance, places) for q in (low, up, rhs)]
            low_a, up_a, rhs_a = [shift_pair(q, -distance, places) for q in (low, up, rhs)]
            pivot = add(mul(low, up_b), mul(up, low_a))
            inv = reciprocal((1.0 - pivot[0], -pivot[1]))
            rhs = mul(sub(rhs, add(mul(low, rhs_b), mul(up, rhs_a))), inv)
            if 2 * distance < strips:
                low, up = neg(mul(mul(low, low_b), inv)), neg(mul(mul(up, up_a), inv))
            distance *= 2
        slope = sub(mul(r, shift_pair(rhs, -1, places)), add(mul(a, rhs), inner))
        for i, q in enumerate((rhs[0], rhs[1], slope[0], slope[1])):
            pick_ref[4 * f + i] = q

    state = []
    for f in range(freq_local):
        w_in, d_in = [
            tuple(
                jnp.broadcast_to(pick_ref[4 * f + 2 * i + c, pl.ds(strip, 1), :], (SEGMENTS, lanes))
                for c in range(2)
            )
            for i in range(2)
        ]
        m00, m01, m10, m11, v0, v1 = [
            shift_pair((scan_ref[f, 2 * i], scan_ref[f, 2 * i + 1]), 1, rows) for i in range(6)
        ]
        first = rows == 0
        m00 = (jnp.where(first, 1.0, m00[0]), m00[1])
        m11 = (jnp.where(first, 1.0, m11[0]), m11[1])
        w = add(add(mul(m00, w_in), mul(m01, d_in)), v0)
        d = add(add(mul(m10, w_in), mul(m11, d_in)), v1)
        state.append((w, d))
    for t in range(steps):
        image = None
        vel = vel_ref[core, pl.ds(t, SEGMENTS, stride=steps), :]
        for f in range(freq_local):
            wave = lambda t: (screened_ref[f, 0, t], screened_ref[f, 1, t])
            w, d = state[f]
            out = sub(w, wave(t))
            out_ref[0, f, t] = out[0]
            out_ref[1, f, t] = out[1]
            image = out[0] if image is None else image + out[0]
            if t < steps - 1:
                eps = inverse_kappa(vel, omegas[f])
                d = add(sub(d, mul(eps, w)), source_terms(wave, t, steps, eps, rows))
                state[f] = (add(w, d), d)
        image_ref[pl.ds(t, SEGMENTS, stride=steps), :] = image


def spread(value, axis, count, place):
    index = lax.axis_index(axis)

    def branch(p):
        def run(x):
            at = lambda i: i % count
            far = lax.ppermute(x, axis, [(p, at(p + 2))])
            up = lax.ppermute(x, axis, [(p, at(p + 1))])
            down = lax.ppermute(x, axis, [(p, at(p - 1))])
            return jnp.where(index == p, x, up + far + down)

        return run

    return lax.switch(place, [branch(p) for p in range(count)], value)


def strip_call(kernel, outs, scratch, smem_args, args):
    return pl.pallas_call(
        kernel,
        out_shape=outs,
        in_specs=[pl.BlockSpec(memory_space=pltpu.SMEM)] * smem_args
        + [pl.BlockSpec(memory_space=pltpu.VMEM)] * (len(args) - smem_args),
        out_specs=[pl.BlockSpec(memory_space=pltpu.VMEM)] * len(outs),
        scratch_shapes=scratch,
        compiler_params=pltpu.CompilerParams(vmem_limit_bytes=32 * 1024 * 1024),
    )(*args)


PAIRS_ONE = [(0, 1), (1, 0), (2, 3), (3, 2)]
PAIRS_TWO = [(1, 2), (2, 1), (3, 0), (0, 3)]


def shards(wavefield, velocity_bank, owner):
    freq_local, cells, lanes = wavefield.shape[1:]
    steps = cells // SEGMENTS
    freq_total = freq_local * ZH * YY * CC
    struct = lambda *shape: jax.ShapeDtypeStruct(shape, jnp.float32)
    own = owner[0]
    core = own % CC
    group, half = YY * CC, cells // CC
    home, line = own // group, (own // CC) % YY
    at_home = lax.axis_index("zh") == home

    def share(slab):
        both = lax.all_gather(slab, "c", axis=0)
        return lax.dynamic_slice(both, (core, lax.axis_index("c") * half, 0), (1, half, lanes))[0]

    piece = lax.cond(
        at_home & (lax.axis_index("y") == line), share, lambda slab: slab[:half], velocity_bank[0]
    )
    piece = lax.cond(at_home, lambda x: spread(x, "y", YY, line), lambda x: x, piece)
    piece = spread(piece, "zh", ZH, home)
    velocity = lax.all_gather(piece, "c", axis=0, tiled=True).reshape(1, cells, lanes)
    screened, scan, message = strip_call(
        functools.partial(forward_kernel, freq_total),
        [
            struct(freq_local, 2, steps, SEGMENTS, lanes),
            struct(freq_local, 12, SEGMENTS, lanes),
            struct(MESSAGE, lanes),
        ],
        [],
        1,
        (owner, wavefield, velocity),
    )
    message = jnp.broadcast_to(message, (N_STRIPS, MESSAGE, lanes))
    gathered = lax.all_to_all(message, STRIPS, 0, 0, tiled=True)
    wave_out, partial = strip_call(
        functools.partial(backward_kernel, freq_total),
        [struct(2, freq_local, steps, SEGMENTS, lanes), struct(cells, lanes)],
        [pltpu.VMEM((4 * freq_local, N_STRIPS, lanes), jnp.float32)],
        1,
        (owner, gathered.reshape(N_STRIPS * MESSAGE, lanes), screened, scan, velocity),
    )
    both = lax.all_gather(partial, "c", axis=0)
    begin = lax.axis_index("c") * half
    total = jnp.sum(lax.dynamic_slice(both, (0, begin, 0), (CC, half, lanes)), axis=0)
    total = jnp.sum(
        lax.all_to_all(jnp.broadcast_to(total, (YY, half, lanes)), "y", 0, 0, tiled=True), axis=0
    )
    total = total + lax.ppermute(total, "zh", PAIRS_ONE)
    total = total + lax.ppermute(total, "zh", PAIRS_TWO)
    total = total * (1.0 / math.sqrt(freq_total))
    image = lax.all_gather(total, "c", axis=0, tiled=True)
    wave_out = jnp.swapaxes(wave_out, 2, 3).reshape(wavefield.shape)
    return (wave_out, image.reshape(cells, lanes))


def solution(mesh):
    grid = Mesh(mesh.devices.reshape(ZH, YY, CC, ZL, XX), FREQ + STRIPS)
    return jax.shard_map(
        shards,
        mesh=grid,
        in_specs=(P(None, FREQ, STRIPS, None), P(FREQ, STRIPS, None), P()),
        out_specs=(P(None, FREQ, STRIPS, None), P(STRIPS, None)),
        check_vma=False,
    )
```

```python
import functools
import math

import jax
import jax.numpy as jnp
from jax import lax
from jax.experimental import pallas as pl
from jax.experimental.pallas import tpu as pltpu
from jax.sharding import Mesh, PartitionSpec as P

BETA = 1.0 / 6.0
GAIN = 30000.0
PHASE = 2.0

ZH, YY, CC, ZL, XX = 4, 4, 2, 4, 4
FREQ = ("zh", "y", "c")
STRIPS = ("zl", "x")
N_STRIPS = ZL * XX
SEGMENTS = 8
FIELDS = 7
MESSAGE = 32


def mul(a, b):
    return (a[0] * b[0] - a[1] * b[1], a[0] * b[1] + a[1] * b[0])


def add(a, b):
    return (a[0] + b[0], a[1] + b[1])


def sub(a, b):
    return (a[0] - b[0], a[1] - b[1])


def neg(a):
    return (-a[0], -a[1])


def scale(s, a):
    return (s * a[0], s * a[1])


def reciprocal(a):
    inverse = 1.0 / (a[0] * a[0] + a[1] * a[1])
    return (a[0] * inverse, -a[1] * inverse)


def sin_cos(angle):
    h = 0.5 * angle
    z = h * h
    s = 1.0 / 6227020800.0
    for k in (-1.0 / 39916800.0, 1.0 / 362880.0, -1.0 / 5040.0, 1.0 / 120.0, -1.0 / 6.0):
        s = s * z + k
    s = h + h * (z * s)
    c = 1.0 / 87178291200.0
    c = -c * z + 1.0 / 479001600.0
    for k in (-1.0 / 3628800.0, 1.0 / 40320.0, -1.0 / 720.0, 1.0 / 24.0, -0.5):
        c = c * z + k
    c = 1.0 + z * c
    return 2.0 * s * c, 1.0 - 2.0 * s * s


def inverse_kappa(velocity, angular):
    big = GAIN * velocity * (1.0 / angular)
    inverse = 1.0 / (BETA * BETA + big * big)
    return (BETA * inverse, big * inverse)


def angular_of(f, freq_local, freq_total):
    index = (lax.axis_index("zh") * YY + lax.axis_index("y")) * CC + lax.axis_index("c")
    index = index * freq_local + f
    return 1.0 + 3.0 * index.astype(jnp.float32) / freq_total


def shift_rows(x, distance, rows):
    count = x.shape[0]
    rolled = pltpu.roll(x, distance % count, 0)
    inside = rows >= distance if distance > 0 else rows < count + distance
    return jnp.where(inside, rolled, 0.0)


def shift_pair(a, distance, rows):
    return (shift_rows(a[0], distance, rows), shift_rows(a[1], distance, rows))


def source_terms(wave, t, steps, eps, rows):
    here = wave(t)
    prev = wave(t - 1) if t > 0 else shift_pair(wave(steps - 1), 1, rows)
    after = wave(t + 1) if t < steps - 1 else shift_pair(wave(0), -1, rows)
    lap = sub(add(prev, after), scale(2.0, here))
    return mul(scale(2.0, eps), add(here, scale(BETA, lap)))


def forward_kernel(freq_total, owner_ref, wave_ref, vel_ref, screened_ref, scan_ref, message_ref):
    freq_local, cells = wave_ref.shape[1], wave_ref.shape[2]
    steps = cells // SEGMENTS
    lanes = wave_ref.shape[3]
    core = 0
    rows = lax.broadcasted_iota(jnp.int32, (SEGMENTS, lanes), 0)
    one = jnp.ones((SEGMENTS, lanes), jnp.float32)
    zero = jnp.zeros((SEGMENTS, lanes), jnp.float32)
    omegas = [angular_of(f, freq_local, freq_total) for f in range(freq_local)]

    def velocity(t):
        return vel_ref[core, pl.ds(t, SEGMENTS, stride=steps), :]

    for t in range(steps):
        psi = PHASE * (1.0 / velocity(t) - 1.0 / 3.0)
        for f in range(freq_local):
            sin, cos = sin_cos(omegas[f] * psi)
            re = wave_ref[0, f, pl.ds(t, SEGMENTS, stride=steps), :]
            im = wave_ref[1, f, pl.ds(t, SEGMENTS, stride=steps), :]
            screened_ref[f, 0, t] = re * cos - im * sin
            screened_ref[f, 1, t] = re * sin + im * cos

    message_ref[...] = jnp.zeros(message_ref.shape, jnp.float32)
    for f in range(freq_local):
        wave = lambda t: (screened_ref[f, 0, t], screened_ref[f, 1, t])
        state = [[(one, zero), (zero, zero)], [(zero, zero), (one, zero)], [(zero, zero), (zero, zero)]]
        for t in range(steps):
            eps = inverse_kappa(velocity(t), omegas[f])
            g = source_terms(wave, t, steps, eps, rows)
            for i in range(3):
                w, d = state[i]
                d = sub(d, mul(eps, w))
                if i == 2:
                    d = add(d, g)
                state[i] = [add(w, d), d]
        (m00, m10), (m01, m11), (v0, v1) = state
        distance = 1
        while distance < SEGMENTS:
            b00, b01, b10, b11, bv0, bv1 = [
                (pltpu.roll(q[0], distance, 0), pltpu.roll(q[1], distance, 0))
                for q in (m00, m01, m10, m11, v0, v1)
            ]
            new = (
                add(mul(m00, b00), mul(m01, b10)),
                add(mul(m00, b01), mul(m01, b11)),
                add(mul(m10, b00), mul(m11, b10)),
                add(mul(m10, b01), mul(m11, b11)),
                add(add(mul(m00, bv0), mul(m01, bv1)), v0),
                add(add(mul(m10, bv0), mul(m11, bv1)), v1),
            )
            use = rows >= distance
            m00, m01, m10, m11, v0, v1 = [
                (jnp.where(use, n[0], q[0]), jnp.where(use, n[1], q[1]))
                for n, q in zip(new, (m00, m01, m10, m11, v0, v1))
            ]
            distance *= 2
        for i, q in enumerate((m00, m01, m10, m11, v0, v1)):
            scan_ref[f, 2 * i] = q[0]
            scan_ref[f, 2 * i + 1] = q[1]
        r = reciprocal(m01)
        b = mul(m11, r)
        fields = (r, mul(m00, r), b, mul(r, v0), sub(v1, mul(b, v0)))
        base = f * FIELDS * 2
        for i, q in enumerate(fields):
            for c in range(2):
                message_ref[base + 2 * i + c : base + 2 * i + c + 1, :] = q[c][SEGMENTS - 1 :, :]
        for c in range(2):
            message_ref[base + 10 + c : base + 11 + c, :] = screened_ref[f, c, 0][0:1, :]
            message_ref[base + 12 + c : base + 13 + c, :] = screened_ref[f, c, steps - 1][SEGMENTS - 1 :, :]
    tail = freq_local * FIELDS * 2
    message_ref[tail : tail + 1, :] = velocity(0)[0:1, :]
    message_ref[tail + 1 : tail + 2, :] = velocity(steps - 1)[SEGMENTS - 1 :, :]


def backward_kernel(freq_total, owner_ref, gathered_ref, screened_ref, scan_ref, vel_ref, out_ref, image_ref, pick_ref):
    freq_local, steps, _, lanes = out_ref.shape[1:]
    strips = gathered_ref.shape[0] // MESSAGE
    core = 0
    strip = lax.axis_index("zl") * XX + lax.axis_index("x")
    rows = lax.broadcasted_iota(jnp.int32, (SEGMENTS, lanes), 0)
    places = lax.broadcasted_iota(jnp.int32, (strips, lanes), 0)
    omegas = [angular_of(f, freq_local, freq_total) for f in range(freq_local)]

    def field(i):
        return gathered_ref[pl.ds(i, strips, stride=MESSAGE), :]

    tail = freq_local * FIELDS * 2
    vel_head, vel_tail = field(tail), field(tail + 1)
    for f in range(freq_local):
        base = f * FIELDS * 2
        r, a, b, q0, q1, p_head, p_tail = [
            (field(base + 2 * i), field(base + 2 * i + 1)) for i in range(FIELDS)
        ]
        eps_head = inverse_kappa(vel_head, omegas[f])
        eps_tail = inverse_kappa(vel_tail, omegas[f])
        e = mul(scale(2.0 * BETA, eps_head), shift_pair(p_tail, 1, places))
        c = mul(scale(2.0 * BETA, eps_tail), shift_pair(p_head, -1, places))
        carry = add(q1, sub(c, mul(c, b)))
        inner = add(q0, mul(r, c))
        rhs = add(add(inner, e), shift_pair(carry, 1, places))
        b_below = shift_pair(b, 1, places)
        diag = add(a, (jnp.where(places == 0, 1.0, b_below[0]), b_below[1]))
        inv = neg(reciprocal(diag))
        low = mul(shift_pair(r, 1, places), inv)
        edge = places == strips - 1
        up = mul((jnp.where(edge, 0.0, r[0]), jnp.where(edge, 0.0, r[1])), inv)
        rhs = mul(rhs, inv)
        distance = 1
        while distance < strips:
            low_b, up_b, rhs_b = [shift_pair(q, distance, places) for q in (low, up, rhs)]
            low_a, up_a, rhs_a = [shift_pair(q, -distance, places) for q in (low, up, rhs)]
            pivot = add(mul(low, up_b), mul(up, low_a))
            inv = reciprocal((1.0 - pivot[0], -pivot[1]))
            rhs = mul(sub(rhs, add(mul(low, rhs_b), mul(up, rhs_a))), inv)
            if 2 * distance < strips:
                low, up = neg(mul(mul(low, low_b), inv)), neg(mul(mul(up, up_a), inv))
            distance *= 2
        slope = sub(mul(r, shift_pair(rhs, -1, places)), add(mul(a, rhs), inner))
        for i, q in enumerate((rhs[0], rhs[1], slope[0], slope[1])):
            pick_ref[4 * f + i] = q

    state = []
    for f in range(freq_local):
        w_in, d_in = [
            tuple(
                jnp.broadcast_to(pick_ref[4 * f + 2 * i + c, pl.ds(strip, 1), :], (SEGMENTS, lanes))
                for c in range(2)
            )
            for i in range(2)
        ]
        m00, m01, m10, m11, v0, v1 = [
            shift_pair((scan_ref[f, 2 * i], scan_ref[f, 2 * i + 1]), 1, rows) for i in range(6)
        ]
        first = rows == 0
        m00 = (jnp.where(first, 1.0, m00[0]), m00[1])
        m11 = (jnp.where(first, 1.0, m11[0]), m11[1])
        w = add(add(mul(m00, w_in), mul(m01, d_in)), v0)
        d = add(add(mul(m10, w_in), mul(m11, d_in)), v1)
        state.append((w, d))
    for t in range(steps):
        image = None
        vel = vel_ref[core, pl.ds(t, SEGMENTS, stride=steps), :]
        for f in range(freq_local):
            wave = lambda t: (screened_ref[f, 0, t], screened_ref[f, 1, t])
            w, d = state[f]
            out = sub(w, wave(t))
            out_ref[0, f, t] = out[0]
            out_ref[1, f, t] = out[1]
            image = out[0] if image is None else image + out[0]
            if t < steps - 1:
                eps = inverse_kappa(vel, omegas[f])
                d = add(sub(d, mul(eps, w)), source_terms(wave, t, steps, eps, rows))
                state[f] = (add(w, d), d)
        image_ref[pl.ds(t, SEGMENTS, stride=steps), :] = image


def spread(value, axis, count, place):
    index = lax.axis_index(axis)

    def branch(p):
        def run(x):
            at = lambda i: i % count
            far = lax.ppermute(x, axis, [(p, at(p + 2))])
            up = lax.ppermute(x, axis, [(p, at(p + 1))])
            down = lax.ppermute(x, axis, [(p, at(p - 1))])
            return jnp.where(index == p, x, up + far + down)

        return run

    return lax.switch(place, [branch(p) for p in range(count)], value)


def strip_call(kernel, outs, scratch, smem_args, args):
    return pl.pallas_call(
        kernel,
        out_shape=outs,
        in_specs=[pl.BlockSpec(memory_space=pltpu.SMEM)] * smem_args
        + [pl.BlockSpec(memory_space=pltpu.VMEM)] * (len(args) - smem_args),
        out_specs=[pl.BlockSpec(memory_space=pltpu.VMEM)] * len(outs),
        scratch_shapes=scratch,
        compiler_params=pltpu.CompilerParams(vmem_limit_bytes=32 * 1024 * 1024),
    )(*args)


PAIRS_ONE = [(0, 1), (1, 0), (2, 3), (3, 2)]
PAIRS_TWO = [(1, 2), (2, 1), (3, 0), (0, 3)]


def shards(wavefield, velocity_bank, owner):
    freq_local, cells, lanes = wavefield.shape[1:]
    steps = cells // SEGMENTS
    freq_total = freq_local * ZH * YY * CC
    struct = lambda *shape: jax.ShapeDtypeStruct(shape, jnp.float32)
    own = owner[0]
    core = own % CC
    group, half = YY * CC, cells // CC
    home, line = own // group, (own // CC) % YY
    at_home = lax.axis_index("zh") == home

    begin = (lax.axis_index("c") * half).astype(jnp.uint32)
    origin = jnp.uint32(0)

    def share(slab, begin):
        both = lax.all_gather(slab, "c", axis=0)
        return lax.dynamic_slice(both, (core.astype(jnp.uint32), begin, origin), (1, half, lanes))[0]

    piece = lax.cond(
        at_home & (lax.axis_index("y") == line),
        share,
        lambda slab, begin: slab[:half],
        velocity_bank[0],
        begin,
    )
    piece = lax.cond(at_home, lambda x: spread(x, "y", YY, line), lambda x: x, piece)
    piece = spread(piece, "zh", ZH, home)
    velocity = lax.all_gather(piece, "c", axis=0, tiled=True).reshape(1, cells, lanes)
    screened, scan, message = strip_call(
        functools.partial(forward_kernel, freq_total),
        [
            struct(freq_local, 2, steps, SEGMENTS, lanes),
            struct(freq_local, 12, SEGMENTS, lanes),
            struct(MESSAGE, lanes),
        ],
        [],
        1,
        (owner, wavefield, velocity),
    )
    message = jnp.broadcast_to(message, (N_STRIPS, MESSAGE, lanes))
    gathered = lax.all_to_all(message, STRIPS, 0, 0, tiled=True)
    wave_out, partial = strip_call(
        functools.partial(backward_kernel, freq_total),
        [struct(2, freq_local, steps, SEGMENTS, lanes), struct(cells, lanes)],
        [pltpu.VMEM((4 * freq_local, N_STRIPS, lanes), jnp.float32)],
        1,
        (owner, gathered.reshape(N_STRIPS * MESSAGE, lanes), screened, scan, velocity),
    )
    both = lax.all_gather(partial, "c", axis=0)
    total = jnp.sum(lax.dynamic_slice(both, (origin, begin, origin), (CC, half, lanes)), axis=0)
    total = jnp.sum(
        lax.all_to_all(jnp.broadcast_to(total, (YY, half, lanes)), "y", 0, 0, tiled=True), axis=0
    )
    total = total + lax.ppermute(total, "zh", PAIRS_ONE)
    total = total + lax.ppermute(total, "zh", PAIRS_TWO)
    total = total * (1.0 / math.sqrt(freq_total))
    image = lax.all_gather(total, "c", axis=0, tiled=True)
    wave_out = jnp.swapaxes(wave_out, 2, 3).reshape(wavefield.shape)
    return (wave_out, image.reshape(cells, lanes))


def solution(mesh):
    grid = Mesh(mesh.devices.reshape(ZH, YY, CC, ZL, XX), FREQ + STRIPS)
    return jax.shard_map(
        shards,
        mesh=grid,
        in_specs=(P(None, FREQ, STRIPS, None), P(FREQ, STRIPS, None), P()),
        out_specs=(P(None, FREQ, STRIPS, None), P(STRIPS, None)),
        check_vma=False,
    )
```

```python
import functools
import math

import jax
import jax.numpy as jnp
from jax import lax
from jax.experimental import pallas as pl
from jax.experimental.pallas import tpu as pltpu
from jax.sharding import Mesh, PartitionSpec as P

BETA = 1.0 / 6.0
GAIN = 30000.0
PHASE = 2.0

ZH, YY, CC, ZL, XX = 4, 4, 2, 4, 4
FREQ = ("zh", "y", "c")
STRIPS = ("zl", "x")
N_STRIPS = ZL * XX
SEGMENTS = 8
FIELDS = 7
MESSAGE = 32


def mul(a, b):
    return (a[0] * b[0] - a[1] * b[1], a[0] * b[1] + a[1] * b[0])


def add(a, b):
    return (a[0] + b[0], a[1] + b[1])


def sub(a, b):
    return (a[0] - b[0], a[1] - b[1])


def neg(a):
    return (-a[0], -a[1])


def scale(s, a):
    return (s * a[0], s * a[1])


def reciprocal(a):
    inverse = 1.0 / (a[0] * a[0] + a[1] * a[1])
    return (a[0] * inverse, -a[1] * inverse)


def sin_cos(angle):
    h = 0.5 * angle
    z = h * h
    s = 1.0 / 6227020800.0
    for k in (-1.0 / 39916800.0, 1.0 / 362880.0, -1.0 / 5040.0, 1.0 / 120.0, -1.0 / 6.0):
        s = s * z + k
    s = h + h * (z * s)
    c = 1.0 / 87178291200.0
    c = -c * z + 1.0 / 479001600.0
    for k in (-1.0 / 3628800.0, 1.0 / 40320.0, -1.0 / 720.0, 1.0 / 24.0, -0.5):
        c = c * z + k
    c = 1.0 + z * c
    return 2.0 * s * c, 1.0 - 2.0 * s * s


def inverse_kappa(velocity, angular):
    big = GAIN * velocity * (1.0 / angular)
    inverse = 1.0 / (BETA * BETA + big * big)
    return (BETA * inverse, big * inverse)


def angular_of(f, freq_local, freq_total):
    index = (lax.axis_index("zh") * YY + lax.axis_index("y")) * CC + lax.axis_index("c")
    index = index * freq_local + f
    return 1.0 + 3.0 * index.astype(jnp.float32) / freq_total


def shift_rows(x, distance, rows):
    count = x.shape[0]
    rolled = pltpu.roll(x, distance % count, 0)
    inside = rows >= distance if distance > 0 else rows < count + distance
    return jnp.where(inside, rolled, 0.0)


def shift_pair(a, distance, rows):
    return (shift_rows(a[0], distance, rows), shift_rows(a[1], distance, rows))


def source_terms(wave, t, steps, eps, rows):
    here = wave(t)
    prev = wave(t - 1) if t > 0 else shift_pair(wave(steps - 1), 1, rows)
    after = wave(t + 1) if t < steps - 1 else shift_pair(wave(0), -1, rows)
    lap = sub(add(prev, after), scale(2.0, here))
    return mul(scale(2.0, eps), add(here, scale(BETA, lap)))


def forward_kernel(freq_total, owner_ref, wave_ref, vel_ref, screened_ref, scan_ref, message_ref):
    freq_local, cells = wave_ref.shape[1], wave_ref.shape[2]
    steps = cells // SEGMENTS
    lanes = wave_ref.shape[3]
    core = 0
    rows = lax.broadcasted_iota(jnp.int32, (SEGMENTS, lanes), 0)
    one = jnp.ones((SEGMENTS, lanes), jnp.float32)
    zero = jnp.zeros((SEGMENTS, lanes), jnp.float32)
    omegas = [angular_of(f, freq_local, freq_total) for f in range(freq_local)]

    def velocity(t):
        return vel_ref[core, pl.ds(t, SEGMENTS, stride=steps), :]

    for t in range(steps):
        psi = PHASE * (1.0 / velocity(t) - 1.0 / 3.0)
        for f in range(freq_local):
            sin, cos = sin_cos(omegas[f] * psi)
            re = wave_ref[0, f, pl.ds(t, SEGMENTS, stride=steps), :]
            im = wave_ref[1, f, pl.ds(t, SEGMENTS, stride=steps), :]
            screened_ref[f, 0, t] = re * cos - im * sin
            screened_ref[f, 1, t] = re * sin + im * cos

    message_ref[...] = jnp.zeros(message_ref.shape, jnp.float32)
    for f in range(freq_local):
        wave = lambda t: (screened_ref[f, 0, t], screened_ref[f, 1, t])
        state = [[(one, zero), (zero, zero)], [(zero, zero), (one, zero)], [(zero, zero), (zero, zero)]]
        for t in range(steps):
            eps = inverse_kappa(velocity(t), omegas[f])
            g = source_terms(wave, t, steps, eps, rows)
            for i in range(3):
                w, d = state[i]
                d = sub(d, mul(eps, w))
                if i == 2:
                    d = add(d, g)
                state[i] = [add(w, d), d]
        (m00, m10), (m01, m11), (v0, v1) = state
        distance = 1
        while distance < SEGMENTS:
            b00, b01, b10, b11, bv0, bv1 = [
                (pltpu.roll(q[0], distance, 0), pltpu.roll(q[1], distance, 0))
                for q in (m00, m01, m10, m11, v0, v1)
            ]
            new = (
                add(mul(m00, b00), mul(m01, b10)),
                add(mul(m00, b01), mul(m01, b11)),
                add(mul(m10, b00), mul(m11, b10)),
                add(mul(m10, b01), mul(m11, b11)),
                add(add(mul(m00, bv0), mul(m01, bv1)), v0),
                add(add(mul(m10, bv0), mul(m11, bv1)), v1),
            )
            use = rows >= distance
            m00, m01, m10, m11, v0, v1 = [
                (jnp.where(use, n[0], q[0]), jnp.where(use, n[1], q[1]))
                for n, q in zip(new, (m00, m01, m10, m11, v0, v1))
            ]
            distance *= 2
        for i, q in enumerate((m00, m01, m10, m11, v0, v1)):
            scan_ref[f, 2 * i] = q[0]
            scan_ref[f, 2 * i + 1] = q[1]
        r = reciprocal(m01)
        b = mul(m11, r)
        fields = (r, mul(m00, r), b, mul(r, v0), sub(v1, mul(b, v0)))
        base = f * FIELDS * 2
        for i, q in enumerate(fields):
            for c in range(2):
                message_ref[base + 2 * i + c : base + 2 * i + c + 1, :] = q[c][SEGMENTS - 1 :, :]
        for c in range(2):
            message_ref[base + 10 + c : base + 11 + c, :] = screened_ref[f, c, 0][0:1, :]
            message_ref[base + 12 + c : base + 13 + c, :] = screened_ref[f, c, steps - 1][SEGMENTS - 1 :, :]
    tail = freq_local * FIELDS * 2
    message_ref[tail : tail + 1, :] = velocity(0)[0:1, :]
    message_ref[tail + 1 : tail + 2, :] = velocity(steps - 1)[SEGMENTS - 1 :, :]


def backward_kernel(freq_total, owner_ref, gathered_ref, screened_ref, scan_ref, vel_ref, out_ref, image_ref, pick_ref):
    freq_local, steps, _, lanes = out_ref.shape[1:]
    strips = gathered_ref.shape[0] // MESSAGE
    core = 0
    strip = lax.axis_index("zl") * XX + lax.axis_index("x")
    rows = lax.broadcasted_iota(jnp.int32, (SEGMENTS, lanes), 0)
    places = lax.broadcasted_iota(jnp.int32, (strips, lanes), 0)
    omegas = [angular_of(f, freq_local, freq_total) for f in range(freq_local)]

    def field(i):
        return gathered_ref[pl.ds(i, strips, stride=MESSAGE), :]

    tail = freq_local * FIELDS * 2
    vel_head, vel_tail = field(tail), field(tail + 1)
    for f in range(freq_local):
        base = f * FIELDS * 2
        r, a, b, q0, q1, p_head, p_tail = [
            (field(base + 2 * i), field(base + 2 * i + 1)) for i in range(FIELDS)
        ]
        eps_head = inverse_kappa(vel_head, omegas[f])
        eps_tail = inverse_kappa(vel_tail, omegas[f])
        e = mul(scale(2.0 * BETA, eps_head), shift_pair(p_tail, 1, places))
        c = mul(scale(2.0 * BETA, eps_tail), shift_pair(p_head, -1, places))
        carry = add(q1, sub(c, mul(c, b)))
        inner = add(q0, mul(r, c))
        rhs = add(add(inner, e), shift_pair(carry, 1, places))
        b_below = shift_pair(b, 1, places)
        diag = add(a, (jnp.where(places == 0, 1.0, b_below[0]), b_below[1]))
        inv = neg(reciprocal(diag))
        low = mul(shift_pair(r, 1, places), inv)
        edge = places == strips - 1
        up = mul((jnp.where(edge, 0.0, r[0]), jnp.where(edge, 0.0, r[1])), inv)
        rhs = mul(rhs, inv)
        distance = 1
        while distance < strips:
            low_b, up_b, rhs_b = [shift_pair(q, distance, places) for q in (low, up, rhs)]
            low_a, up_a, rhs_a = [shift_pair(q, -distance, places) for q in (low, up, rhs)]
            pivot = add(mul(low, up_b), mul(up, low_a))
            inv = reciprocal((1.0 - pivot[0], -pivot[1]))
            rhs = mul(sub(rhs, add(mul(low, rhs_b), mul(up, rhs_a))), inv)
            if 2 * distance < strips:
                low, up = neg(mul(mul(low, low_b), inv)), neg(mul(mul(up, up_a), inv))
            distance *= 2
        slope = sub(mul(r, shift_pair(rhs, -1, places)), add(mul(a, rhs), inner))
        for i, q in enumerate((rhs[0], rhs[1], slope[0], slope[1])):
            pick_ref[4 * f + i] = q

    state = []
    for f in range(freq_local):
        w_in, d_in = [
            tuple(
                jnp.broadcast_to(pick_ref[4 * f + 2 * i + c, pl.ds(strip, 1), :], (SEGMENTS, lanes))
                for c in range(2)
            )
            for i in range(2)
        ]
        m00, m01, m10, m11, v0, v1 = [
            shift_pair((scan_ref[f, 2 * i], scan_ref[f, 2 * i + 1]), 1, rows) for i in range(6)
        ]
        first = rows == 0
        m00 = (jnp.where(first, 1.0, m00[0]), m00[1])
        m11 = (jnp.where(first, 1.0, m11[0]), m11[1])
        w = add(add(mul(m00, w_in), mul(m01, d_in)), v0)
        d = add(add(mul(m10, w_in), mul(m11, d_in)), v1)
        state.append((w, d))
    for t in range(steps):
        image = None
        vel = vel_ref[core, pl.ds(t, SEGMENTS, stride=steps), :]
        for f in range(freq_local):
            wave = lambda t: (screened_ref[f, 0, t], screened_ref[f, 1, t])
            w, d = state[f]
            out = sub(w, wave(t))
            out_ref[0, f, t] = out[0]
            out_ref[1, f, t] = out[1]
            image = out[0] if image is None else image + out[0]
            if t < steps - 1:
                eps = inverse_kappa(vel, omegas[f])
                d = add(sub(d, mul(eps, w)), source_terms(wave, t, steps, eps, rows))
                state[f] = (add(w, d), d)
        image_ref[pl.ds(t, SEGMENTS, stride=steps), :] = image


def spread(value, axis, count, place):
    index = lax.axis_index(axis)

    def branch(p):
        def run(x):
            at = lambda i: i % count
            far = lax.ppermute(x, axis, [(p, at(p + 2))])
            up = lax.ppermute(x, axis, [(p, at(p + 1))])
            down = lax.ppermute(x, axis, [(p, at(p - 1))])
            return jnp.where(index == p, x, up + far + down)

        return run

    return lax.switch(place, [branch(p) for p in range(count)], value)


def strip_call(kernel, outs, scratch, smem_args, args):
    return pl.pallas_call(
        kernel,
        out_shape=outs,
        in_specs=[pl.BlockSpec(memory_space=pltpu.SMEM)] * smem_args
        + [pl.BlockSpec(memory_space=pltpu.VMEM)] * (len(args) - smem_args),
        out_specs=[pl.BlockSpec(memory_space=pltpu.VMEM)] * len(outs),
        scratch_shapes=scratch,
        compiler_params=pltpu.CompilerParams(vmem_limit_bytes=32 * 1024 * 1024),
    )(*args)


PAIRS_ONE = [(0, 1), (1, 0), (2, 3), (3, 2)]
PAIRS_TWO = [(1, 2), (2, 1), (3, 0), (0, 3)]


def shards(wavefield, velocity_bank, owner):
    freq_local, cells, lanes = wavefield.shape[1:]
    steps = cells // SEGMENTS
    freq_total = freq_local * ZH * YY * CC
    struct = lambda *shape: jax.ShapeDtypeStruct(shape, jnp.float32)
    own = owner[0]
    core = own % CC
    group, half = YY * CC, cells // CC
    home, line = own // group, (own // CC) % YY
    at_home = lax.axis_index("zh") == home

    begin = (lax.axis_index("c") * half).astype(jnp.uint32)
    origin, other = jnp.uint32(0), jnp.uint32(half) - begin

    def share(slab, begin, other):
        both = lax.all_gather(slab, "c", axis=0)
        return lax.dynamic_slice(both, (core.astype(jnp.uint32), begin, origin), (1, half, lanes))[0]

    piece = lax.cond(
        at_home & (lax.axis_index("y") == line),
        share,
        lambda slab, begin, other: lax.dynamic_slice(slab, (other, origin), (half, lanes)),
        velocity_bank[0],
        begin,
        other,
    )
    piece = lax.cond(at_home, lambda x: spread(x, "y", YY, line), lambda x: x, piece)
    piece = spread(piece, "zh", ZH, home)
    velocity = lax.all_gather(piece, "c", axis=0, tiled=True).reshape(1, cells, lanes)
    screened, scan, message = strip_call(
        functools.partial(forward_kernel, freq_total),
        [
            struct(freq_local, 2, steps, SEGMENTS, lanes),
            struct(freq_local, 12, SEGMENTS, lanes),
            struct(MESSAGE, lanes),
        ],
        [],
        1,
        (owner, wavefield, velocity),
    )
    message = jnp.broadcast_to(message, (N_STRIPS, MESSAGE, lanes))
    gathered = lax.all_to_all(message, STRIPS, 0, 0, tiled=True)
    wave_out, partial = strip_call(
        functools.partial(backward_kernel, freq_total),
        [struct(2, freq_local, steps, SEGMENTS, lanes), struct(cells, lanes)],
        [pltpu.VMEM((4 * freq_local, N_STRIPS, lanes), jnp.float32)],
        1,
        (owner, gathered.reshape(N_STRIPS * MESSAGE, lanes), screened, scan, velocity),
    )
    rows_at = lambda array, place: lax.dynamic_slice(array, (place, origin), (half, lanes))
    both = lax.all_gather(rows_at(partial, other), "c", axis=0, tiled=True)
    total = rows_at(partial, begin) + rows_at(both, other)
    total = jnp.sum(
        lax.all_to_all(jnp.broadcast_to(total, (YY, half, lanes)), "y", 0, 0, tiled=True), axis=0
    )
    total = total + lax.ppermute(total, "zh", PAIRS_ONE)
    total = total + lax.ppermute(total, "zh", PAIRS_TWO)
    total = total * (1.0 / math.sqrt(freq_total))
    image = lax.all_gather(total, "c", axis=0, tiled=True)
    wave_out = jnp.swapaxes(wave_out, 2, 3).reshape(wavefield.shape)
    return (wave_out, image.reshape(cells, lanes))


def solution(mesh):
    grid = Mesh(mesh.devices.reshape(ZH, YY, CC, ZL, XX), FREQ + STRIPS)
    return jax.shard_map(
        shards,
        mesh=grid,
        in_specs=(P(None, FREQ, STRIPS, None), P(FREQ, STRIPS, None), P()),
        out_specs=(P(None, FREQ, STRIPS, None), P(STRIPS, None)),
        check_vma=False,
    )
```
